256 devices in a mesh: gx: 8 (over x, core), gy: 8 (over z), gz: 4 (over y).
Axes of the slice: x: 4, y: 4, z: 8, core: 2. Of those that a mesh axis runs over, the one named last changes fastest.
Arguments:
- positions: float32 [3, 16, 16, 16, 128], P(None, 'gx', 'gy', 'gz'), may hold values from 0 to 11
- velocities: float32 [3, 16, 16, 16, 128], P(None, 'gx', 'gy', 'gz'), may hold values from -0.6 to 0.6
- counts: int32 [16, 16, 16], P('gx', 'gy', 'gz'), may hold values from 96 to 128
Outputs:
- new_velocity: float32 [3, 16, 16, 16, 128], P(None, 'gx', 'gy', 'gz')
- moved: float32 [3, 16, 16, 16, 128], P(None, 'gx', 'gy', 'gz')
The draws below stay inside these ranges and needn't reach their ends.
All inputs are finite; a program needn't handle non-finite values.
Results may differ from the reference program's by a relative error of at most 0.0003.
Values sent between devices are 32-bit elements; how exact they have to be, the bound alone decides.
A program may use at most 64 MiB of HBM per device.

```python
import jax
import jax.numpy as jnp
from jax import lax

SLOTS = 128
STEPS = 1
NX = 16
NY = 16
NZ = 16


def set_ends(result, key, low, largest):
    place = [jax.random.randint(jax.random.fold_in(key, axis), (), 0, length) for axis, length in enumerate(result.shape)]
    longest = result.shape.index(max(result.shape))
    next_to = place[:longest] + [(place[longest] + 1) % result.shape[longest]] + place[longest + 1:]
    return result.at[tuple(place)].set(low).at[tuple(next_to)].set(largest)


def steps_of(stream_key, shape, split, least, high):
    def one(axis_at, parts):
        heights = jax.random.uniform(jax.random.fold_in(jax.random.fold_in(stream_key, 6), axis_at), (parts,), jnp.float32, least / len(split), high / len(split))
        return jnp.repeat(jnp.exp(heights), shape[axis_at] // parts).reshape((-1,) + (1,) * (len(shape) - axis_at - 1))

    loudness = one(*split[0])
    for cut in split[1:]:
        loudness = loudness * one(*cut)
    return loudness


def gaussian(stream_key, dims, width, bound, cuts=(), kind=jnp.bfloat16):
    entries = width * jax.random.normal(stream_key, dims, jnp.float32)
    if cuts:
        entries = entries * steps_of(stream_key, dims, cuts, -0.22, 0.18)
    return jnp.clip(entries, -bound, bound).astype(kind)


def setup_inputs(seed: int = 0) -> dict:
    seeds = jax.random.split(jax.random.key(seed), 4)
    positions = jnp.clip(11.0 * jax.random.uniform(seeds[0], (3, NX, NY, NZ, SLOTS), jnp.float32) ** steps_of(seeds[0], (3, NX, NY, NZ, SLOTS), ((1, 8), (2, 8), (3, 4)), -0.2, 0.2), 0.0, 11.0)
    velocities = gaussian(seeds[1], (3, NX, NY, NZ, SLOTS), 0.1, 0.6, ((1, 8), (2, 8), (3, 4)), jnp.float32)
    counts = set_ends(jax.random.randint(seeds[2], (NX, NY, NZ), SLOTS - SLOTS // 4, SLOTS + 1), jax.random.fold_in(seeds[2], 1), SLOTS - SLOTS // 4, SLOTS).astype(jnp.int32)
    return {"positions": positions, "velocities": velocities, "counts": counts}


CELL_EDGE = 11.0
CUT_SQ = 25.0
WIDTH_DENSITY = 4.0
WIDTH_PAIR = 2.0
SCALE_DENSITY = 0.4
SCALE_PAIR = 0.3
DENSITY_REF = 1.0
TIME_STEP = 0.5
BOX_PAIRS = (
    ((0, 0, 0), (1, 0, 0)), ((0, 0, 0), (0, 1, 0)), ((0, 0, 0), (0, 0, 1)),
    ((0, 0, 0), (1, 1, 0)), ((0, 0, 0), (1, 0, 1)), ((0, 0, 0), (0, 1, 1)),
    ((0, 0, 0), (1, 1, 1)), ((0, 1, 0), (1, 0, 0)), ((0, 0, 1), (1, 0, 0)),
    ((0, 0, 1), (0, 1, 0)), ((0, 1, 0), (1, 0, 1)), ((0, 0, 1), (1, 1, 0)),
    ((1, 0, 0), (0, 1, 1)),
)


def smooth_parts(radius_sq):
    inside = radius_sq < CUT_SQ
    remain = 1.0 - radius_sq / CUT_SQ
    smooth = jnp.where(inside, remain * remain, 0.0)
    smooth_slope = jnp.where(inside, -2.0 * remain / CUT_SQ, 0.0)
    return smooth, smooth_slope


def separation_of(slab_a, slab_b, offset):
    shift_vec = jnp.array(offset, jnp.float32) * CELL_EDGE
    return slab_b[:, :, None, :] - slab_a[:, :, :, None] + shift_vec[:, None, None, None]


def tile_weight(mask_a, mask_b, self_tile):
    weight = mask_a[:, :, None] * mask_b[:, None, :]
    if self_tile:
        weight = weight * (1.0 - jnp.eye(mask_a.shape[1], dtype=mask_a.dtype))
    return weight


def pair_density(slab_a, slab_b, mask_a, mask_b, offset, self_tile):
    separation = separation_of(slab_a, slab_b, offset)
    radius_sq = jnp.sum(separation * separation, axis=0)
    smooth, unused_slope = smooth_parts(radius_sq)
    pair_term = tile_weight(mask_a, mask_b, self_tile) * SCALE_DENSITY * jnp.exp(-radius_sq / WIDTH_DENSITY) * smooth
    return jnp.sum(pair_term, axis=2), jnp.sum(pair_term, axis=1)


def pair_force(slab_a, slab_b, mask_a, mask_b, grad_a, grad_b, offset, self_tile):
    separation = separation_of(slab_a, slab_b, offset)
    radius_sq = jnp.sum(separation * separation, axis=0)
    smooth, smooth_slope = smooth_parts(radius_sq)
    density_fall = SCALE_DENSITY * jnp.exp(-radius_sq / WIDTH_DENSITY)
    density_slope = density_fall * (smooth_slope - smooth / WIDTH_DENSITY)
    pair_fall = SCALE_PAIR * jnp.exp(-radius_sq / WIDTH_PAIR)
    pair_slope = pair_fall * (smooth_slope - smooth / WIDTH_PAIR)
    factor = tile_weight(mask_a, mask_b, self_tile) * 2.0 * (
        pair_slope + (grad_a[:, :, None] + grad_b[:, None, :]) * density_slope)
    pushed = factor[None] * separation
    return jnp.sum(pushed, axis=3), -jnp.sum(pushed, axis=2)


def pick_block(cell_count, most):
    for candidate in range(most, 0, -1):
        if cell_count % candidate == 0:
            return candidate
    return 1


def take_cells(field, first_cell, block_size, axis_index):
    return lax.dynamic_slice_in_dim(field, first_cell, block_size, axis_index)


def density_sweep(slab_a, slab_b, mask_a, mask_b, offset, self_tile, most):
    cell_count, slot_count = mask_a.shape
    block_size = pick_block(cell_count, most)
    empty_sums = jnp.zeros((cell_count, slot_count), mask_a.dtype)

    def visit_block(block_index, running):
        row_sums, col_sums = running
        first_cell = (block_index * block_size).astype(jnp.int32)
        row_block, col_block = pair_density(
            take_cells(slab_a, first_cell, block_size, 1), take_cells(slab_b, first_cell, block_size, 1),
            take_cells(mask_a, first_cell, block_size, 0), take_cells(mask_b, first_cell, block_size, 0),
            offset, self_tile)
        row_sums = lax.dynamic_update_slice_in_dim(row_sums, row_block, first_cell, 0)
        col_sums = lax.dynamic_update_slice_in_dim(col_sums, col_block, first_cell, 0)
        return row_sums, col_sums

    return lax.fori_loop(0, cell_count // block_size, visit_block, (empty_sums, empty_sums))


def force_sweep(slab_a, slab_b, mask_a, mask_b, grad_a, grad_b, offset, self_tile, most):
    cell_count, slot_count = mask_a.shape
    block_size = pick_block(cell_count, most)
    empty_push = jnp.zeros((3, cell_count, slot_count), mask_a.dtype)

    def visit_block(block_index, running):
        push_a, push_b = running
        first_cell = (block_index * block_size).astype(jnp.int32)
        block_a, block_b = pair_force(
            take_cells(slab_a, first_cell, block_size, 1), take_cells(slab_b, first_cell, block_size, 1),
            take_cells(mask_a, first_cell, block_size, 0), take_cells(mask_b, first_cell, block_size, 0),
            take_cells(grad_a, first_cell, block_size, 0), take_cells(grad_b, first_cell, block_size, 0),
            offset, self_tile)
        push_a = lax.dynamic_update_slice_in_dim(push_a, block_a, first_cell, 1)
        push_b = lax.dynamic_update_slice_in_dim(push_b, block_b, first_cell, 1)
        return push_a, push_b

    return lax.fori_loop(0, cell_count // block_size, visit_block, (empty_push, empty_push))


def moved_cells(field, corner):
    return jnp.roll(field, shift=(-corner[0], -corner[1], -corner[2]), axis=(-4, -3, -2))


def restore_cells(field, corner):
    return jnp.roll(field, shift=(corner[0], corner[1], corner[2]), axis=(-4, -3, -2))


def total_forces(positions, live):
    grid_shape = live.shape
    cell_count = grid_shape[0] * grid_shape[1] * grid_shape[2]
    slot_count = grid_shape[3]
    flat_pos = positions.reshape(3, cell_count, slot_count)
    flat_live = live.reshape(cell_count, slot_count)
    row_block, unused_cols = density_sweep(flat_pos, flat_pos, flat_live, flat_live, (0, 0, 0), True, 64)
    density = row_block.reshape(grid_shape)
    for corner_a, corner_b in BOX_PAIRS:
        offset = (corner_b[0] - corner_a[0], corner_b[1] - corner_a[1], corner_b[2] - corner_a[2])
        pos_a = moved_cells(positions, corner_a).reshape(3, cell_count, slot_count)
        pos_b = moved_cells(positions, corner_b).reshape(3, cell_count, slot_count)
        live_a = moved_cells(live, corner_a).reshape(cell_count, slot_count)
        live_b = moved_cells(live, corner_b).reshape(cell_count, slot_count)
        row_block, col_block = density_sweep(pos_a, pos_b, live_a, live_b, offset, False, 64)
        density = density + restore_cells(row_block.reshape(grid_shape), corner_a)
        density = density + restore_cells(col_block.reshape(grid_shape), corner_b)
    embed_grad = live * 2.0 * (density - DENSITY_REF)
    flat_grad = embed_grad.reshape(cell_count, slot_count)
    push_a, unused_push = force_sweep(flat_pos, flat_pos, flat_live, flat_live, flat_grad, flat_grad, (0, 0, 0), True, 64)
    forces = push_a.reshape(positions.shape)
    for corner_a, corner_b in BOX_PAIRS:
        offset = (corner_b[0] - corner_a[0], corner_b[1] - corner_a[1], corner_b[2] - corner_a[2])
        pos_a = moved_cells(positions, corner_a).reshape(3, cell_count, slot_count)
        pos_b = moved_cells(positions, corner_b).reshape(3, cell_count, slot_count)
        live_a = moved_cells(live, corner_a).reshape(cell_count, slot_count)
        live_b = moved_cells(live, corner_b).reshape(cell_count, slot_count)
        grad_a = moved_cells(embed_grad, corner_a).reshape(cell_count, slot_count)
        grad_b = moved_cells(embed_grad, corner_b).reshape(cell_count, slot_count)
        push_a, push_b = force_sweep(pos_a, pos_b, live_a, live_b, grad_a, grad_b, offset, False, 64)
        forces = forces + restore_cells(push_a.reshape(positions.shape), corner_a)
        forces = forces + restore_cells(push_b.reshape(positions.shape), corner_b)
    return forces


def live_slots(counts, slot_count):
    slot_index = lax.broadcasted_iota(jnp.int32, counts.shape + (slot_count,), 3)
    return (slot_index < counts[..., None].astype(jnp.int32)).astype(jnp.float32)


def reference(positions, velocities, counts):
    live = live_slots(counts, positions.shape[4])
    running_position = positions
    running_velocity = velocities
    for moment in range(STEPS):
        forces = total_forces(running_position, live)
        running_velocity = running_velocity + TIME_STEP * forces
        running_position = running_position + TIME_STEP * running_velocity
    return running_velocity * live[None], (running_position - positions) * live[None]
```

```python
import functools
import math

import jax
import jax.numpy as jnp
from jax import lax
from jax.experimental import pallas as pl
from jax.experimental.pallas import tpu as pltpu
from jax.sharding import PartitionSpec as P

MESH = pl.DeviceIdType.MESH
EDGE = 11.0
BETA = math.log2(math.e) / 4.0
ALPHA = 25.0 * BETA
DEAD = -30000.0
RHO_SHIFT = 8.0 * ALPHA / 25.0
PAIR_SHIFT = 4.0 * ALPHA / 25.0
RHO_SCALE = 0.4 * 2.0 ** (-ALPHA) / ALPHA**2
RHO_SLOPE_SCALE = -0.1 * 2.0 ** (-ALPHA) / ALPHA**2
PAIR_SLOPE_SCALE = -0.15 * 2.0 ** (-2.0 * ALPHA) / ALPHA**2
TIME_STEP = 0.5
OFFSETS = [
    (dx, dy, dz)
    for dx in (-1, 0, 1)
    for dy in (-1, 0, 1)
    for dz in (-1, 0, 1)
    if (dx, dy, dz) != (0, 0, 0)
]
OWN = (2, 2, 4)
EXT = (4, 4, 6)
CELLS = OWN[0] * OWN[1] * OWN[2]
EXT_CELLS = EXT[0] * EXT[1] * EXT[2]
F32, BF16 = jnp.float32, jnp.bfloat16


def source_slice(step, size):
    if step == 0:
        return pl.ds(1, size)
    return pl.ds(size if step > 0 else 1, 1)


def target_slice(step, size):
    if step == 0:
        return pl.ds(1, size)
    return pl.ds(0 if step > 0 else size + 1, 1)


def round16(value):
    return value.astype(BF16).astype(F32)


def split3(value):
    high = round16(value)
    rest = value - high
    low = round16(rest)
    return high, low, rest - low


def kernel(
    pos_ref, vel_ref, cnt_ref, vout_ref, mout_ref,
    ext, gext, lhs, mom, gmom, wts, accp, slopes,
    send_sem, recv_sem, gsend_sem, grecv_sem,
):
    sizes = [lax.axis_size(name) for name in ("gx", "gy", "gz")]
    me = [lax.axis_index(name) for name in ("gx", "gy", "gz")]

    def neighbour(offset):
        return tuple(lax.rem(m + d + n, n) for m, d, n in zip(me, offset, sizes))

    barrier = pltpu.get_barrier_semaphore()
    for offset in OFFSETS:
        pl.semaphore_signal(barrier, inc=1, device_id=neighbour(offset), device_id_type=MESH)

    lane = lax.broadcasted_iota(jnp.int32, (1, 128), 1)
    for x in range(OWN[0]):
        for y in range(OWN[1]):
            for z in range(OWN[2]):
                for c in range(3):
                    ext[1 + x, 1 + y, 1 + z, c : c + 1, :] = (
                        pos_ref[c, x, y, z : z + 1, :] - 0.5 * EDGE
                    )
                live = jnp.where(lane < cnt_ref[x, y, z], 1.0, 0.0)
                ext[1 + x, 1 + y, 1 + z, 3:4, :] = live

    pl.semaphore_wait(barrier, len(OFFSETS))

    def exchange(buffer, sends, recvs):
        copies = []
        for k, offset in enumerate(OFFSETS):
            src = tuple(source_slice(d, n) for d, n in zip(offset, OWN))
            dst = tuple(target_slice(d, n) for d, n in zip(offset, OWN))
            copy = pltpu.make_async_remote_copy(
                src_ref=buffer.at[src],
                dst_ref=buffer.at[dst],
                send_sem=sends.at[k],
                recv_sem=recvs.at[k],
                device_id=neighbour(offset),
                device_id_type=MESH,
            )
            copy.start()
            copies.append(copy)
        return copies

    copies = exchange(ext, send_sem, recv_sem)
    row4 = lax.broadcasted_iota(jnp.int32, (4, 128), 0)

    def shifted(x, y, z):
        cx = (x.astype(F32) - 1.5) * EDGE
        cy = (y.astype(F32) - 1.5) * EDGE
        cz = (z.astype(F32) - 2.5) * EDGE
        centre = jnp.where(row4 == 0, cx, jnp.where(row4 == 1, cy, jnp.where(row4 == 2, cz, 0.0)))
        return ext[x, y, z] + centre

    def norm_of(point):
        square = point * point
        total = square[0:1] + square[1:2] + square[2:3]
        return jnp.where(point[3:4] > 0.5, -BETA * total, DEAD)

    def own_step(i, carry):
        x, y, z = i // 8, lax.rem(i // 4, 2), lax.rem(i, 4)
        point = shifted(x + 1, y + 1, z + 1)
        high, low, rest = split3(jnp.where(row4 == 3, 1.0, (2.0 * BETA) * point))
        n_high, n_low, n_rest = split3(norm_of(point) + ALPHA)
        norm = jnp.where(row4 == 0, n_high, jnp.where(row4 == 1, n_low, jnp.where(row4 == 2, n_rest, 0.0)))
        wts[i] = jnp.concatenate(
            [high, low, rest, high, low, high, norm, jnp.zeros_like(norm)], axis=0
        ).astype(BF16)
        return carry

    lax.fori_loop(0, CELLS, own_step, 0)

    for copy in copies:
        copy.wait()

    def expand_step(j, carry):
        x, y, z = j // 24, lax.rem(j // 6, 4), lax.rem(j, 6)
        point = shifted(x, y, z)
        full = jnp.where(row4 == 3, norm_of(point), point)
        high, low, rest = split3(full)
        ones = jnp.ones_like(high)
        stack = jnp.concatenate([high, high, high, low, low, rest, ones, jnp.zeros_like(ones)], axis=0)
        lhs[j] = stack.T.astype(BF16)
        moments = jnp.concatenate([high, low, rest, ones], axis=0).astype(BF16)
        mom[j] = jnp.concatenate([moments, moments], axis=1)
        return carry

    lax.fori_loop(0, EXT_CELLS, expand_step, 0)

    eye = lax.broadcasted_iota(jnp.int32, (128, 128), 0) == lax.broadcasted_iota(jnp.int32, (128, 128), 1)

    def cell_base(i):
        return i // 8, lax.rem(i // 4, 2), lax.rem(i, 4)

    def pair_step(i, carry):
        x, y, z = cell_base(i)
        weight = wts[i]
        total = jnp.zeros((8, 128), F32)
        push = jnp.zeros((16, 128), F32)
        for k in range(27):
            dx, dy, dz = k // 9, k // 3 % 3, k % 3
            j = ((x + dx) * 4 + (y + dy)) * 6 + z + dz
            t = jnp.dot(lhs[j], weight, preferred_element_type=F32)
            remain = jnp.maximum(t, 0.0)
            if k == 13:
                remain = jnp.where(eye, 0.0, remain)
            fall = jnp.exp2(t)
            part = remain * fall
            rho = part * remain
            total = total + jnp.sum(rho.reshape(16, 8, 128), axis=0)
            slope = part * (remain + RHO_SHIFT)
            high = slope.astype(BF16)
            slopes[i * 27 + k, 0:128, :] = high
            slopes[i * 27 + k, 128:256, :] = (slope - high.astype(F32)).astype(BF16)
            pair = (part * fall) * (remain + PAIR_SHIFT)
            high = pair.astype(BF16)
            low = (pair - high.astype(F32)).astype(BF16)
            push = push + jnp.dot(
                mom[j], jnp.concatenate([high, low], axis=0), preferred_element_type=F32
            )
        density = RHO_SCALE * jnp.sum(total, axis=0, keepdims=True)
        live = ext[x + 1, y + 1, z + 1, 3:4, :]
        gext[x + 1, y + 1, z + 1] = live * 2.0 * (density - 1.0)
        accp[i] = push
        return carry

    lax.fori_loop(0, CELLS, pair_step, 0)

    copies = exchange(gext, gsend_sem, grecv_sem)
    for copy in copies:
        copy.wait()

    def grad_step(j, carry):
        x, y, z = j // 24, lax.rem(j // 6, 4), lax.rem(j, 6)
        point = jnp.where(row4 == 3, 1.0, shifted(x, y, z))
        high, low, rest = split3(point * gext[x, y, z])
        moments = jnp.concatenate([high, low, rest, jnp.zeros_like(rest)], axis=0).astype(BF16)
        gmom[j, 0:16, :] = mom[j]
        gmom[j, 16:32, :] = jnp.concatenate([moments, moments], axis=1)
        return carry

    lax.fori_loop(0, EXT_CELLS, grad_step, 0)

    def force_step(i, carry):
        x, y, z = cell_base(i)
        total = jnp.zeros((32, 128), F32)
        for k in range(27):
            dx, dy, dz = k // 9, k // 3 % 3, k % 3
            j = ((x + dx) * 4 + (y + dy)) * 6 + z + dz
            total = total + jnp.dot(gmom[j], slopes[i * 27 + k], preferred_element_type=F32)
        push = accp[i]
        point = shifted(x + 1, y + 1, z + 1)
        grad = gext[x + 1, y + 1, z + 1]
        live = point[3:4]

        def net(block, count):
            return block[0:4] + block[4:8] + block[8:12] - point * count

        pair_part = net(push, push[12:13])
        own_part = net(total[0:16], total[12:13])
        block = total[16:32]
        other_part = net(block, block[3:4] + block[7:8] + block[11:12])
        force = 2.0 * (
            PAIR_SLOPE_SCALE * pair_part + RHO_SLOPE_SCALE * (grad * own_part + other_part)
        )
        for c in range(3):
            place = pos_ref[c, x, y, pl.ds(z, 1), :]
            velocity = vel_ref[c, x, y, pl.ds(z, 1), :] + TIME_STEP * force[c : c + 1]
            vout_ref[c, x, y, pl.ds(z, 1), :] = velocity * live
            mout_ref[c, x, y, pl.ds(z, 1), :] = ((place + TIME_STEP * velocity) - place) * live
        return carry

    lax.fori_loop(0, CELLS, force_step, 0)


def body(positions, velocities, counts):
    vmem = pl.BlockSpec(memory_space=pltpu.VMEM)
    shape = jax.ShapeDtypeStruct(positions.shape, F32)
    links = len(OFFSETS)
    return pl.pallas_call(
        kernel,
        out_shape=(shape, shape),
        in_specs=[vmem, vmem, pl.BlockSpec(memory_space=pltpu.SMEM)],
        out_specs=(vmem, vmem),
        scratch_shapes=[
            pltpu.VMEM(EXT + (4, 128), F32),
            pltpu.VMEM(EXT + (1, 128), F32),
            pltpu.VMEM((EXT_CELLS, 128, 32), BF16),
            pltpu.VMEM((EXT_CELLS, 16, 256), BF16),
            pltpu.VMEM((EXT_CELLS, 32, 256), BF16),
            pltpu.VMEM((CELLS, 32, 128), BF16),
            pltpu.VMEM((CELLS, 16, 128), F32),
            pltpu.VMEM((CELLS * 27, 256, 128), BF16),
            pltpu.SemaphoreType.DMA((links,)),
            pltpu.SemaphoreType.DMA((links,)),
            pltpu.SemaphoreType.DMA((links,)),
            pltpu.SemaphoreType.DMA((links,)),
        ],
        compiler_params=pltpu.CompilerParams(
            collective_id=0, has_side_effects=True, vmem_limit_bytes=48 * 1024 * 1024
        ),
    )(positions, velocities, counts)


def solution(mesh):
    spec = P(None, "gx", "gy", "gz", None)
    return jax.shard_map(
        body,
        mesh=mesh,
        in_specs=(spec, spec, P("gx", "gy", "gz")),
        out_specs=(spec, spec),
        check_vma=False,
    )
```

```python
import functools
import math

import jax
import jax.numpy as jnp
from jax import lax
from jax.experimental import pallas as pl
from jax.experimental.pallas import tpu as pltpu
from jax.sharding import PartitionSpec as P

MESH = pl.DeviceIdType.MESH
EDGE = 11.0
BETA = math.log2(math.e) / 4.0
ALPHA = 25.0 * BETA
DEAD = -30000.0
SHIFT = 4.0 * ALPHA / 25.0
RHO_SCALE = 0.4 * 2.0 ** (-ALPHA) / ALPHA**2
FORCE_SCALE = 2.0 * -0.15 * 2.0 ** (-2.0 * ALPHA) / ALPHA**2
GRAD_SCALE = 2.0 / 3.0 * 2.0**ALPHA
TIME_STEP = 0.5
OFFSETS = [
    (dx, dy, dz)
    for dx in (-1, 0, 1)
    for dy in (-1, 0, 1)
    for dz in (-1, 0, 1)
    if (dx, dy, dz) != (0, 0, 0)
]
OWN = (2, 2, 4)
EXT = (4, 4, 6)
CELLS = OWN[0] * OWN[1] * OWN[2]
COLUMNS = EXT[0] * EXT[1]
GRAD_ROWS = 8 * EXT[2]
F32, BF16 = jnp.float32, jnp.bfloat16


def source_slice(step, size):
    if step == 0:
        return pl.ds(1, size)
    return pl.ds(size if step > 0 else 1, 1)


def target_slice(step, size):
    if step == 0:
        return pl.ds(1, size)
    return pl.ds(0 if step > 0 else size + 1, 1)


def round16(value):
    return value.astype(BF16).astype(F32)


def split3(value):
    high = round16(value)
    rest = value - high
    low = round16(rest)
    return high, low, rest - low


def kernel(
    pos_hbm, vel_hbm, cnt_hbm, vout_ref, mout_ref,
    pos_ref, vel_ref, cnt_ref, ext, gext, lhs, mom, wts, pwts, gwide, grow, wide, single, dens, push,
    load_sem, send_sem, recv_sem, gsend_sem, grecv_sem,
):
    loads = [
        pltpu.make_async_copy(source, target, load_sem.at[k])
        for k, (source, target) in enumerate(
            ((pos_hbm, pos_ref), (cnt_hbm, cnt_ref), (vel_hbm, vel_ref))
        )
    ]
    for load in loads:
        load.start()

    sizes = [lax.axis_size(name) for name in ("gx", "gy", "gz")]
    me = [lax.axis_index(name) for name in ("gx", "gy", "gz")]

    def neighbour(offset):
        return tuple(lax.rem(m + d + n, n) for m, d, n in zip(me, offset, sizes))

    barrier = pltpu.get_barrier_semaphore()
    for offset in OFFSETS:
        pl.semaphore_signal(barrier, inc=1, device_id=neighbour(offset), device_id_type=MESH)

    for load in loads:
        load.wait()
    lane = lax.broadcasted_iota(jnp.int32, (1, 128), 1)
    for x in range(OWN[0]):
        for y in range(OWN[1]):
            for z in range(OWN[2]):
                for c in range(3):
                    ext[1 + x, 1 + y, 1 + z, c : c + 1, :] = (
                        pos_ref[c, x, y, z : z + 1, :] - 0.5 * EDGE
                    )
                live = jnp.where(lane < cnt_ref[x, y, z], 1.0, 0.0)
                ext[1 + x, 1 + y, 1 + z, 3:4, :] = live

    pl.semaphore_wait(barrier, len(OFFSETS))

    def exchange(buffer, sends, recvs):
        copies = []
        for k, offset in enumerate(OFFSETS):
            src = tuple(source_slice(d, n) for d, n in zip(offset, OWN))
            dst = tuple(target_slice(d, n) for d, n in zip(offset, OWN))
            copy = pltpu.make_async_remote_copy(
                src_ref=buffer.at[src],
                dst_ref=buffer.at[dst],
                send_sem=sends.at[k],
                recv_sem=recvs.at[k],
                device_id=neighbour(offset),
                device_id_type=MESH,
            )
            copy.start()
            copies.append(copy)
        return copies

    copies = exchange(ext, send_sem, recv_sem)
    row4 = lax.broadcasted_iota(jnp.int32, (4, 128), 0)

    def by_row(values):
        result = jnp.zeros((4, 128), F32)
        for k, value in enumerate(values):
            result = jnp.where(row4 == k, value, result)
        return result

    def shifted(x, y, z):
        cx = (x.astype(F32) - 1.5) * EDGE
        cy = (y.astype(F32) - 1.5) * EDGE
        cz = (z - 2.5) * EDGE
        return ext[x, y, z] + by_row((cx, cy, cz))

    def norm_of(point):
        square = point * point
        total = square[0:1] + square[1:2] + square[2:3]
        return jnp.where(point[3:4] > 0.5, -BETA * total, DEAD)

    def expand(x, y, z):
        point = shifted(x, y, z)
        norm = norm_of(point)
        high, low, rest = split3(jnp.where(row4 == 3, norm, point))
        ones = jnp.ones_like(high)
        stack = jnp.concatenate([high, high, high, low, low, rest, ones, jnp.zeros_like(ones)], axis=0)
        j = (x * 4 + y, z)
        lhs[j] = stack.T.astype(BF16)
        moments = jnp.concatenate([high, low, rest, ones], axis=0).astype(BF16)
        mom[j] = jnp.concatenate([moments, moments], axis=1)
        return point, norm

    def pair_columns(k):
        side = lax.rem(k, 2)
        return jnp.where(k < 2, 2 * side, side), jnp.where(k < 2, 2 * side + 1, side + 2)

    def own_column(q):
        return 1 + q // 2, 1 + lax.rem(q, 2)

    def own_step(q, carry):
        x, y = own_column(q)
        for z in range(4):
            point, norm = expand(x, y, z + 1)
            high, low, rest = split3(jnp.where(row4 == 3, 1.0, (2.0 * BETA) * point))
            pieces = by_row(split3(norm + ALPHA))
            wts[q * 4 + z] = jnp.concatenate(
                [high, low, rest, high, low, high, pieces, jnp.zeros_like(pieces)], axis=0
            ).astype(BF16)
        return carry

    lax.fori_loop(0, 4, own_step, 0)

    def pair_step(k, carry):
        first, second = pair_columns(k)
        for z in range(4):
            pwts[k * 4 + z] = jnp.concatenate([wts[first * 4 + z], wts[second * 4 + z]], axis=1)
        return carry

    lax.fori_loop(0, 4, pair_step, 0)

    eye = lax.broadcasted_iota(jnp.int32, (128, 128), 0) == lax.broadcasted_iota(jnp.int32, (128, 128), 1)
    own_pairs = [(iz, jz) for iz in range(4) for jz in range(1, 5) if abs(iz + 1 - jz) <= 1]
    edge_pairs = [(0, 0), (3, 5)]
    all_pairs = [(iz, iz + dz) for iz in range(4) for dz in range(3)]

    def density_tile(j, weight, masked, store, slot):
        t = jnp.dot(lhs[j], weight, preferred_element_type=F32)
        width = t.shape[1]
        remain = jnp.maximum(t, 0.0)
        if masked is not None:
            halves = [remain[:, h * 128 : h * 128 + 128] for h in range(width // 128)]
            halves[masked] = jnp.where(eye, 0.0, halves[masked])
            remain = jnp.concatenate(halves, axis=1)
        part = remain * jnp.exp2(t)
        store[slot] = part
        return jnp.sum((part * remain).reshape(16, 8, width), axis=0)

    def force_tile(j, weight, grad, store, slot):
        t = jnp.dot(lhs[j], weight, preferred_element_type=F32)
        width = t.shape[1]
        column, z = j
        other = gwide[column, :, z * 128 : z * 128 + 128]
        if width == 256:
            other = jnp.concatenate([other, other], axis=1)
        both = other + grad
        factor = store[slot] * ((t + SHIFT) * (jnp.exp2(t) + both) + SHIFT * both)
        high = factor.astype(BF16)
        low = (factor - high.astype(F32)).astype(BF16)
        return jnp.dot(mom[j], jnp.concatenate([high, low], axis=0), preferred_element_type=F32)

    def group(kind, bases, weights, items, store, slot, first=False):
        totals = {}
        for n, (column, iz, jz, masked) in enumerate(items):
            j = (column, jz)
            weight = weights(iz)
            if kind == "density":
                part = density_tile(j, weight, masked, store, slot + n)
            else:
                grad = jnp.concatenate([grow[base + iz] for base in bases], axis=1)
                part = force_tile(j, weight, grad, store, slot + n)
            totals[iz] = part if iz not in totals else totals[iz] + part
        target = dens if kind == "density" else push
        for iz, total in totals.items():
            for h, base in enumerate(bases):
                block = total[:, h * 128 : h * 128 + 128]
                target[base + iz] = block if first else target[base + iz] + block

    def pair_group(kind, k, items, slot, first=False):
        one, two = pair_columns(k)
        group(kind, [one * 4, two * 4], lambda iz: pwts[k * 4 + iz], items, wide, slot, first)

    def own_part(kind):
        def same_step(k, carry):
            columns = [(1 + k) * 4 + y for y in (1, 2)]
            items = [
                (column, iz, jz, h if jz == iz + 1 else None)
                for h, column in enumerate(columns)
                for iz, jz in own_pairs
            ]
            pair_group(kind, k, items, k * 20, True)
            return carry

        def other_step(p, carry):
            k = p // 2
            column = (2 - k) * 4 + 1 + lax.rem(p, 2)
            pair_group(kind, k, [(column, iz, jz, None) for iz, jz in own_pairs], 40 + p * 10)
            return carry

        lax.fori_loop(0, 2, same_step, 0)
        lax.fori_loop(0, 4, other_step, 0)

    def halo_part(kind):
        def edge_step(k, carry):
            items = [(c, iz, jz, None) for c in (5, 6, 9, 10) for iz, jz in edge_pairs]
            pair_group(kind, k, items, 80 + k * 8)
            return carry

        def face_step(p, carry):
            k, far = p // 2, lax.rem(p, 2)
            side = 1 + lax.rem(k, 2)
            near = k < 2
            column = jnp.where(near, 4 * (3 * (side - 1)) + 1 + far, 4 * (1 + far) + 3 * (side - 1))
            pair_group(kind, k, [(column, iz, jz, None) for iz, jz in all_pairs], 96 + p * 12)
            return carry

        def corner_step(q, carry):
            column = 12 * (q // 2) + 3 * lax.rem(q, 2)
            group(
                kind, [q * 4], lambda iz: wts[q * 4 + iz],
                [(column, iz, jz, None) for iz, jz in all_pairs], single, q * 12,
            )
            return carry

        lax.fori_loop(0, 2, edge_step, 0)
        lax.fori_loop(0, 8, face_step, 0)
        lax.fori_loop(0, 4, corner_step, 0)

    def halo_column(k):
        x = jnp.where(k < 4, 0, jnp.where(k < 8, 3, 1 + lax.rem(k, 2)))
        y = jnp.where(k < 8, lax.rem(k, 4), jnp.where(k < 10, 0, 3))
        return x, y

    own_part("density")

    for copy in copies:
        copy.wait()

    def halo_expand(k, carry):
        x, y = halo_column(k)
        for z in range(6):
            expand(x, y, z)
        return carry

    def edge_expand(q, carry):
        x, y = own_column(q)
        expand(x, y, 0)
        expand(x, y, 5)
        return carry

    lax.fori_loop(0, 4, edge_expand, 0)
    lax.fori_loop(0, 12, halo_expand, 0)

    halo_part("density")

    def grad_step(q, carry):
        x, y = own_column(q)
        for z in range(4):
            density = RHO_SCALE * jnp.sum(dens[q * 4 + z], axis=0, keepdims=True)
            gext[x, y, z + 1] = ext[x, y, z + 1, 3:4, :] * 2.0 * (density - 1.0)
        return carry

    lax.fori_loop(0, 4, grad_step, 0)
    copies = exchange(gext, gsend_sem, grecv_sem)

    row8 = lax.broadcasted_iota(jnp.int32, (8, 128), 0)

    def grad_column(x, y, inner):
        rows = []
        for z in range(6):
            if inner and z in (0, 5):
                rows.append(jnp.zeros((8, 128), F32))
                continue
            high, low, rest = split3(GRAD_SCALE * gext[x, y, z])
            rows.append(
                jnp.where(row8 == 0, high, jnp.where(row8 == 1, low, jnp.where(row8 == 2, rest, 0.0)))
            )
        turned = jnp.concatenate(rows, axis=0).T.astype(BF16)
        gwide[x * 4 + y] = jnp.dot(turned, spread, preferred_element_type=F32)

    spread_row = lax.broadcasted_iota(jnp.int32, (GRAD_ROWS, 768), 0) // 8
    spread_lane = lax.broadcasted_iota(jnp.int32, (GRAD_ROWS, 768), 1) // 128
    spread = jnp.where(spread_row == spread_lane, 1.0, 0.0).astype(BF16)

    def own_grad(q, carry):
        x, y = own_column(q)
        for z in range(4):
            grow[q * 4 + z] = GRAD_SCALE * gext[x, y, z + 1]
        grad_column(x, y, True)
        return carry

    lax.fori_loop(0, 4, own_grad, 0)

    own_part("force")

    for copy in copies:
        copy.wait()

    def halo_grad(k, carry):
        x, y = halo_column(k)
        grad_column(x, y, False)
        return carry

    def edge_grad(q, carry):
        x, y = own_column(q)
        grad_column(x, y, False)
        return carry

    lax.fori_loop(0, 4, edge_grad, 0)
    lax.fori_loop(0, 12, halo_grad, 0)

    halo_part("force")

    def finish(q, carry):
        x, y = own_column(q)
        for z in range(4):
            total = push[q * 4 + z]
            point = shifted(x, y, z + 1)
            live = point[3:4]
            force = FORCE_SCALE * (total[0:4] + total[4:8] + total[8:12] - point * total[12:13])
            for c in range(3):
                place = pos_ref[c, x - 1, y - 1, z : z + 1, :]
                velocity = vel_ref[c, x - 1, y - 1, z : z + 1, :] + TIME_STEP * force[c : c + 1]
                vout_ref[c, x - 1, y - 1, z : z + 1, :] = velocity * live
                mout_ref[c, x - 1, y - 1, z : z + 1, :] = (
                    (place + TIME_STEP * velocity) - place
                ) * live
        return carry

    lax.fori_loop(0, 4, finish, 0)


def body(positions, velocities, counts):
    vmem = pl.BlockSpec(memory_space=pltpu.VMEM)
    hbm = pl.BlockSpec(memory_space=pltpu.HBM)
    shape = jax.ShapeDtypeStruct(positions.shape, F32)
    links = len(OFFSETS)
    return pl.pallas_call(
        kernel,
        out_shape=(shape, shape),
        in_specs=[hbm, hbm, hbm],
        out_specs=(vmem, vmem),
        scratch_shapes=[
            pltpu.VMEM(positions.shape, F32),
            pltpu.VMEM(positions.shape, F32),
            pltpu.SMEM(counts.shape, jnp.int32),
            pltpu.VMEM(EXT + (4, 128), F32),
            pltpu.VMEM(EXT + (1, 128), F32),
            pltpu.VMEM((COLUMNS, 6, 128, 32), BF16),
            pltpu.VMEM((COLUMNS, 6, 16, 256), BF16),
            pltpu.VMEM((CELLS, 32, 128), BF16),
            pltpu.VMEM((CELLS, 32, 256), BF16),
            pltpu.VMEM((COLUMNS, 128, 768), F32),
            pltpu.VMEM((CELLS, 1, 128), F32),
            pltpu.VMEM((192, 128, 256), F32),
            pltpu.VMEM((48, 128, 128), F32),
            pltpu.VMEM((CELLS, 8, 128), F32),
            pltpu.VMEM((CELLS, 16, 128), F32),
            pltpu.SemaphoreType.DMA((3,)),
            pltpu.SemaphoreType.DMA((links,)),
            pltpu.SemaphoreType.DMA((links,)),
            pltpu.SemaphoreType.DMA((links,)),
            pltpu.SemaphoreType.DMA((links,)),
        ],
        compiler_params=pltpu.CompilerParams(
            collective_id=0, has_side_effects=True, vmem_limit_bytes=56 * 1024 * 1024
        ),
    )(positions, velocities, counts)


def solution(mesh):
    spec = P(None, "gx", "gy", "gz", None)
    return jax.shard_map(
        body,
        mesh=mesh,
        in_specs=(spec, spec, P("gx", "gy", "gz")),
        out_specs=(spec, spec),
        check_vma=False,
    )
```

```python
import functools
import math

import jax
import jax.numpy as jnp
from jax import lax
from jax.experimental import pallas as pl
from jax.experimental.pallas import tpu as pltpu
from jax.sharding import PartitionSpec as P

MESH = pl.DeviceIdType.MESH
EDGE = 11.0
LOG2E = math.log2(math.e)
PEAK = 25.0 / 4.0
DEAD = -30000.0
RHO_SCALE = 0.4 * math.exp(-PEAK) / PEAK**2
FORCE_SCALE = 2.0 * -0.15 * math.exp(-2.0 * PEAK) / PEAK**2
GRAD_SCALE = 2.0 / 3.0 * math.exp(PEAK)
TIME_STEP = 0.5
OFFSETS = [
    (dx, dy, dz)
    for dx in (-1, 0, 1)
    for dy in (-1, 0, 1)
    for dz in (-1, 0, 1)
    if (dx, dy, dz) != (0, 0, 0)
]
OWN = (2, 2, 4)
EXT = (4, 4, 6)
CELLS = OWN[0] * OWN[1] * OWN[2]
COLUMNS = EXT[0] * EXT[1]
GRAD_ROWS = 8 * EXT[2]
F32, BF16 = jnp.float32, jnp.bfloat16


def source_slice(step, size):
    if step == 0:
        return pl.ds(1, size)
    return pl.ds(size if step > 0 else 1, 1)


def target_slice(step, size):
    if step == 0:
        return pl.ds(1, size)
    return pl.ds(0 if step > 0 else size + 1, 1)


def round16(value):
    return value.astype(BF16).astype(F32)


def split3(value):
    high = round16(value)
    rest = value - high
    low = round16(rest)
    return high, low, rest - low


def kernel(
    pos_hbm, vel_hbm, cnt_hbm, vout_ref, mout_ref,
    pos_ref, vel_ref, cnt_ref, ext, gext, lhs, mom, wts, pwts, gwide, grow, own_part_a, wide_p, wide_r, single_p, single_r, dens, push,
    load_sem, send_sem, recv_sem, gsend_sem, grecv_sem,
):
    loads = [
        pltpu.make_async_copy(source, target, load_sem.at[k])
        for k, (source, target) in enumerate(
            ((pos_hbm, pos_ref), (cnt_hbm, cnt_ref), (vel_hbm, vel_ref))
        )
    ]
    for load in loads:
        load.start()

    sizes = [lax.axis_size(name) for name in ("gx", "gy", "gz")]
    me = [lax.axis_index(name) for name in ("gx", "gy", "gz")]

    def neighbour(offset):
        return tuple(lax.rem(m + d + n, n) for m, d, n in zip(me, offset, sizes))

    barrier = pltpu.get_barrier_semaphore()
    for offset in OFFSETS:
        pl.semaphore_signal(barrier, inc=1, device_id=neighbour(offset), device_id_type=MESH)

    for load in loads:
        load.wait()
    lane = lax.broadcasted_iota(jnp.int32, (1, 128), 1)
    for x in range(OWN[0]):
        for y in range(OWN[1]):
            for z in range(OWN[2]):
                for c in range(3):
                    ext[1 + x, 1 + y, 1 + z, c : c + 1, :] = (
                        pos_ref[c, x, y, z : z + 1, :] - 0.5 * EDGE
                    )
                live = jnp.where(lane < cnt_ref[x, y, z], 1.0, 0.0)
                ext[1 + x, 1 + y, 1 + z, 3:4, :] = live

    pl.semaphore_wait(barrier, len(OFFSETS))

    def exchange(buffer, sends, recvs):
        copies = []
        for k, offset in enumerate(OFFSETS):
            src = tuple(source_slice(d, n) for d, n in zip(offset, OWN))
            dst = tuple(target_slice(d, n) for d, n in zip(offset, OWN))
            copy = pltpu.make_async_remote_copy(
                src_ref=buffer.at[src],
                dst_ref=buffer.at[dst],
                send_sem=sends.at[k],
                recv_sem=recvs.at[k],
                device_id=neighbour(offset),
                device_id_type=MESH,
            )
            copy.start()
            copies.append(copy)
        return copies

    copies = exchange(ext, send_sem, recv_sem)
    row4 = lax.broadcasted_iota(jnp.int32, (4, 128), 0)

    def by_row(values):
        result = jnp.zeros((4, 128), F32)
        for k, value in enumerate(values):
            result = jnp.where(row4 == k, value, result)
        return result

    def shifted(x, y, z):
        cx = (x - 1.5) * EDGE
        cy = (y - 1.5) * EDGE
        cz = (z - 2.5) * EDGE
        return ext[x, y, z] + by_row((cx, cy, cz))

    def norm_of(point):
        square = point * point
        total = square[0:1] + square[1:2] + square[2:3]
        return jnp.where(point[3:4] > 0.5, -0.25 * total, DEAD)

    def expand(x, y, z):
        point = shifted(x, y, z)
        norm = norm_of(point)
        high, low, rest = split3(jnp.where(row4 == 3, norm, point))
        ones = jnp.ones_like(high)
        stack = jnp.concatenate([high, high, high, low, low, rest, ones, jnp.zeros_like(ones)], axis=0)
        j = (x * 4 + y, z)
        lhs[j] = stack.T.astype(BF16)
        moments = jnp.concatenate([high, low, rest, ones], axis=0).astype(BF16)
        mom[j] = jnp.concatenate([moments, moments], axis=1)
        return point, norm

    def pair_columns(k):
        side = lax.rem(k, 2)
        return jnp.where(k < 2, 2 * side, side), jnp.where(k < 2, 2 * side + 1, side + 2)

    def own_column(q):
        return 1 + q // 2, 1 + lax.rem(q, 2)

    def own_step(q, carry):
        x, y = own_column(q)
        for z in range(4):
            point, norm = expand(x, y, z + 1)
            blocks = []
            for unit in (LOG2E, 1.0):
                high, low, rest = split3(jnp.where(row4 == 3, unit, (0.5 * unit) * point))
                pieces = by_row(split3(unit * (norm + PEAK)))
                blocks.append(
                    jnp.concatenate(
                        [high, low, rest, high, low, high, pieces, jnp.zeros_like(pieces)], axis=0
                    )
                )
            wts[q * 4 + z] = jnp.concatenate(blocks, axis=1).astype(BF16)
        return carry

    lax.fori_loop(0, 4, own_step, 0)

    def pair_step(k, carry):
        first, second = pair_columns(k)
        for z in range(4):
            one, two = wts[first * 4 + z], wts[second * 4 + z]
            pwts[k * 4 + z] = jnp.concatenate(
                [one[:, 0:128], two[:, 0:128], one[:, 128:256], two[:, 128:256]], axis=1
            )
        return carry

    lax.fori_loop(0, 4, pair_step, 0)

    eye = lax.broadcasted_iota(jnp.int32, (128, 128), 0) == lax.broadcasted_iota(jnp.int32, (128, 128), 1)
    own_pairs = [(iz, jz) for iz in range(4) for jz in range(1, 5) if abs(iz + 1 - jz) <= 1]
    edge_pairs = [(0, 0), (3, 5)]
    all_pairs = [(iz, iz + dz) for iz in range(4) for dz in range(3)]

    def density_tile(j, weight, masked, stores, slot):
        both = jnp.dot(lhs[j], weight, preferred_element_type=F32)
        width = both.shape[1] // 2
        fall = jnp.exp2(both[:, 0:width])
        remain = jnp.maximum(both[:, width:], 0.0)
        if masked is not None:
            halves = [remain[:, h * 128 : h * 128 + 128] for h in range(width // 128)]
            halves[masked] = jnp.where(eye, 0.0, halves[masked])
            remain = jnp.concatenate(halves, axis=1)
        part = remain * fall
        rho = part * remain
        if len(stores) == 1:
            stores[0][slot] = part
        else:
            mixed = rho + part
            stores[0][slot] = mixed * fall
            stores[1][slot] = mixed + part
        return jnp.sum(rho.reshape(16, 8, width), axis=0)

    def force_tile(j, weight, grad, stores, slot):
        width = grad.shape[1]
        column, z = j
        other = gwide[column, :, z * 128 : z * 128 + 128]
        if width == 256:
            other = jnp.concatenate([other, other], axis=1)
        sums = other + grad
        if len(stores) == 1:
            both = jnp.dot(lhs[j], weight, preferred_element_type=F32)
            fall = jnp.exp2(both[:, 0:width])
            factor = stores[0][slot] * ((both[:, width:] + 1.0) * (fall + sums) + sums)
        else:
            factor = stores[0][slot] + stores[1][slot] * sums
        high = factor.astype(BF16)
        low = (factor - high.astype(F32)).astype(BF16)
        return jnp.dot(mom[j], jnp.concatenate([high, low], axis=0), preferred_element_type=F32)

    def group(kind, bases, weights, items, stores, slot, first=False):
        totals = {}
        for n, (column, iz, jz, masked) in enumerate(items):
            j = (column, jz)
            weight = weights(iz)
            if kind == "density":
                part = density_tile(j, weight, masked, stores, slot + n)
            else:
                grad = jnp.concatenate([grow[base + iz] for base in bases], axis=1)
                part = force_tile(j, weight, grad, stores, slot + n)
            totals[iz] = part if iz not in totals else totals[iz] + part
        target = dens if kind == "density" else push
        for iz, total in totals.items():
            for h, base in enumerate(bases):
                block = total[:, h * 128 : h * 128 + 128]
                target[base + iz] = block if first else target[base + iz] + block

    def pair_group(kind, k, items, stores, slot, first=False):
        one, two = pair_columns(k)
        group(kind, [one * 4, two * 4], lambda iz: pwts[k * 4 + iz], items, stores, slot, first)

    def own_part(kind):
        def same_step(k, carry):
            columns = [(1 + k) * 4 + y for y in (1, 2)]
            items = [
                (column, iz, jz, h if jz == iz + 1 else None)
                for h, column in enumerate(columns)
                for iz, jz in own_pairs
            ]
            pair_group(kind, k, items, [own_part_a], k * 20, True)
            return carry

        def other_step(p, carry):
            k = p // 2
            column = (2 - k) * 4 + 1 + lax.rem(p, 2)
            pair_group(kind, k, [(column, iz, jz, None) for iz, jz in own_pairs], [own_part_a], 40 + p * 10)
            return carry

        lax.fori_loop(0, 2, same_step, 0)
        lax.fori_loop(0, 4, other_step, 0)

    def halo_part(kind):
        def edge_step(k, carry):
            items = [(c, iz, jz, None) for c in (5, 6, 9, 10) for iz, jz in edge_pairs]
            pair_group(kind, k, items, [wide_p, wide_r], k * 8)
            return carry

        def face_step(p, carry):
            k, far = p // 2, lax.rem(p, 2)
            side = 1 + lax.rem(k, 2)
            near = k < 2
            column = jnp.where(near, 4 * (3 * (side - 1)) + 1 + far, 4 * (1 + far) + 3 * (side - 1))
            pair_group(kind, k, [(column, iz, jz, None) for iz, jz in all_pairs], [wide_p, wide_r], 16 + p * 12)
            return carry

        def corner_step(q, carry):
            column = 12 * (q // 2) + 3 * lax.rem(q, 2)
            group(
                kind, [q * 4], lambda iz: wts[q * 4 + iz],
                [(column, iz, jz, None) for iz, jz in all_pairs], [single_p, single_r], q * 12,
            )
            return carry

        lax.fori_loop(0, 2, edge_step, 0)
        lax.fori_loop(0, 8, face_step, 0)
        lax.fori_loop(0, 4, corner_step, 0)

    def halo_column(k):
        x = jnp.where(k < 4, 0, jnp.where(k < 8, 3, 1 + lax.rem(k, 2)))
        y = jnp.where(k < 8, lax.rem(k, 4), jnp.where(k < 10, 0, 3))
        return x, y

    own_part("density")

    for copy in copies:
        copy.wait()

    def halo_expand(k, carry):
        for n in range(2):
            x, y = halo_column(2 * k + n)
            for z in range(6):
                expand(x, y, z)
        return carry

    def edge_expand(q, carry):
        x = q + 1
        for y in (1, 2):
            expand(x, y, 0)
            expand(x, y, 5)
        return carry

    lax.fori_loop(0, 2, edge_expand, 0)
    lax.fori_loop(0, 6, halo_expand, 0)

    halo_part("density")

    def grad_step(q, carry):
        x, y = own_column(q)
        for z in range(4):
            density = RHO_SCALE * jnp.sum(dens[q * 4 + z], axis=0, keepdims=True)
            gext[x, y, z + 1] = ext[x, y, z + 1, 3:4, :] * 2.0 * (density - 1.0)
        return carry

    lax.fori_loop(0, 4, grad_step, 0)
    copies = exchange(gext, gsend_sem, grecv_sem)

    row8 = lax.broadcasted_iota(jnp.int32, (8, 128), 0)

    def grad_column(x, y, inner):
        rows = []
        for z in range(6):
            if inner and z in (0, 5):
                rows.append(jnp.zeros((8, 128), F32))
                continue
            high, low, rest = split3(GRAD_SCALE * gext[x, y, z])
            rows.append(
                jnp.where(row8 == 0, high, jnp.where(row8 == 1, low, jnp.where(row8 == 2, rest, 0.0)))
            )
        turned = jnp.concatenate(rows, axis=0).T.astype(BF16)
        gwide[x * 4 + y] = jnp.dot(turned, spread, preferred_element_type=F32)

    spread_row = lax.broadcasted_iota(jnp.int32, (GRAD_ROWS, 768), 0) // 8
    spread_lane = lax.broadcasted_iota(jnp.int32, (GRAD_ROWS, 768), 1) // 128
    spread = jnp.where(spread_row == spread_lane, 1.0, 0.0).astype(BF16)

    for q in range(4):
        for z in range(4):
            grow[q * 4 + z] = GRAD_SCALE * gext[1 + q // 2, 1 + q % 2, z + 1]
        grad_column(1 + q // 2, 1 + q % 2, True)

    own_part("force")

    for copy in copies:
        copy.wait()

    def row_grad(x, carry):
        for y in range(4):
            grad_column(x, y, False)
        return carry

    lax.fori_loop(0, 4, row_grad, 0)

    halo_part("force")

    def finish(q, carry):
        x, y = own_column(q)
        for z in range(4):
            total = push[q * 4 + z]
            point = shifted(x, y, z + 1)
            live = point[3:4]
            force = FORCE_SCALE * (total[0:4] + total[4:8] + total[8:12] - point * total[12:13])
            for c in range(3):
                place = pos_ref[c, x - 1, y - 1, z : z + 1, :]
                velocity = vel_ref[c, x - 1, y - 1, z : z + 1, :] + TIME_STEP * force[c : c + 1]
                vout_ref[c, x - 1, y - 1, z : z + 1, :] = velocity * live
                mout_ref[c, x - 1, y - 1, z : z + 1, :] = (
                    (place + TIME_STEP * velocity) - place
                ) * live
        return carry

    lax.fori_loop(0, 4, finish, 0)


def body(positions, velocities, counts):
    vmem = pl.BlockSpec(memory_space=pltpu.VMEM)
    hbm = pl.BlockSpec(memory_space=pltpu.HBM)
    shape = jax.ShapeDtypeStruct(positions.shape, F32)
    links = len(OFFSETS)
    return pl.pallas_call(
        kernel,
        out_shape=(shape, shape),
        in_specs=[hbm, hbm, hbm],
        out_specs=(vmem, vmem),
        scratch_shapes=[
            pltpu.VMEM(positions.shape, F32),
            pltpu.VMEM(positions.shape, F32),
            pltpu.SMEM(counts.shape, jnp.int32),
            pltpu.VMEM(EXT + (4, 128), F32),
            pltpu.VMEM(EXT + (1, 128), F32),
            pltpu.VMEM((COLUMNS, 6, 128, 32), BF16),
            pltpu.VMEM((COLUMNS, 6, 16, 256), BF16),
            pltpu.VMEM((CELLS, 32, 256), BF16),
            pltpu.VMEM((CELLS, 32, 512), BF16),
            pltpu.VMEM((COLUMNS, 128, 768), F32),
            pltpu.VMEM((CELLS, 1, 128), F32),
            pltpu.VMEM((80, 128, 256), F32),
            pltpu.VMEM((112, 128, 256), F32),
            pltpu.VMEM((112, 128, 256), F32),
            pltpu.VMEM((48, 128, 128), F32),
            pltpu.VMEM((48, 128, 128), F32),
            pltpu.VMEM((CELLS, 8, 128), F32),
            pltpu.VMEM((CELLS, 16, 128), F32),
            pltpu.SemaphoreType.DMA((3,)),
            pltpu.SemaphoreType.DMA((links,)),
            pltpu.SemaphoreType.DMA((links,)),
            pltpu.SemaphoreType.DMA((links,)),
            pltpu.SemaphoreType.DMA((links,)),
        ],
        compiler_params=pltpu.CompilerParams(
            collective_id=0, has_side_effects=True, vmem_limit_bytes=60 * 1024 * 1024
        ),
    )(positions, velocities, counts)


def solution(mesh):
    spec = P(None, "gx", "gy", "gz", None)
    return jax.shard_map(
        body,
        mesh=mesh,
        in_specs=(spec, spec, P("gx", "gy", "gz")),
        out_specs=(spec, spec),
        check_vma=False,
    )
```

```python
import functools
import math

import jax
import jax.numpy as jnp
from jax import lax
from jax.experimental import pallas as pl
from jax.experimental.pallas import tpu as pltpu
from jax.sharding import PartitionSpec as P

MESH = pl.DeviceIdType.MESH
EDGE = 11.0
LOG2E = math.log2(math.e)
PEAK = 25.0 / 4.0
DEAD = -30000.0
RHO_SCALE = 0.4 * math.exp(-PEAK) / PEAK**2
FORCE_SCALE = 2.0 * -0.15 * math.exp(-2.0 * PEAK) / PEAK**2
GRAD_SCALE = 2.0 / 3.0 * math.exp(PEAK)
TIME_STEP = 0.5
OFFSETS = [
    (dx, dy, dz)
    for dx in (-1, 0, 1)
    for dy in (-1, 0, 1)
    for dz in (-1, 0, 1)
    if (dx, dy, dz) != (0, 0, 0)
]
OWN = (2, 2, 4)
EXT = (4, 4, 6)
CELLS = OWN[0] * OWN[1] * OWN[2]
COLUMNS = EXT[0] * EXT[1]
GRAD_ROWS = 8 * EXT[2]
F32, BF16 = jnp.float32, jnp.bfloat16


def source_slice(step, size):
    if step == 0:
        return pl.ds(1, size)
    return pl.ds(size if step > 0 else 1, 1)


def target_slice(step, size):
    if step == 0:
        return pl.ds(1, size)
    return pl.ds(0 if step > 0 else size + 1, 1)


def round16(value):
    return value.astype(BF16).astype(F32)


def split3(value):
    high = round16(value)
    rest = value - high
    low = round16(rest)
    return high, low, rest - low


def kernel(
    pos_hbm, vel_hbm, cnt_hbm, vout_ref, mout_ref,
    pos_ref, vel_ref, cnt_ref, ext, gext, lhs, mom, wts, pwts, gwide, grow, spread, own_p, own_r, wide_p, wide_r, single_p, single_r, dens, push,
    load_sem, send_sem, recv_sem, gsend_sem, grecv_sem,
):
    loads = [
        pltpu.make_async_copy(source, target, load_sem.at[k])
        for k, (source, target) in enumerate(
            ((pos_hbm, pos_ref), (cnt_hbm, cnt_ref), (vel_hbm, vel_ref))
        )
    ]
    for load in loads:
        load.start()

    sizes = [lax.axis_size(name) for name in ("gx", "gy", "gz")]
    me = [lax.axis_index(name) for name in ("gx", "gy", "gz")]

    def neighbour(offset):
        return tuple(lax.rem(m + d + n, n) for m, d, n in zip(me, offset, sizes))

    barrier = pltpu.get_barrier_semaphore()
    for offset in OFFSETS:
        pl.semaphore_signal(barrier, inc=1, device_id=neighbour(offset), device_id_type=MESH)

    for load in loads:
        load.wait()
    lane = lax.broadcasted_iota(jnp.int32, (1, 128), 1)
    for x in range(OWN[0]):
        for y in range(OWN[1]):
            for z in range(OWN[2]):
                for c in range(3):
                    ext[1 + x, 1 + y, 1 + z, c : c + 1, :] = (
                        pos_ref[c, x, y, z : z + 1, :] - 0.5 * EDGE
                    )
                live = jnp.where(lane < cnt_ref[x, y, z], 1.0, 0.0)
                ext[1 + x, 1 + y, 1 + z, 3:4, :] = live

    pl.semaphore_wait(barrier, len(OFFSETS))

    def exchange(buffer, sends, recvs):
        copies = []
        for k, offset in enumerate(OFFSETS):
            src = tuple(source_slice(d, n) for d, n in zip(offset, OWN))
            dst = tuple(target_slice(d, n) for d, n in zip(offset, OWN))
            copy = pltpu.make_async_remote_copy(
                src_ref=buffer.at[src],
                dst_ref=buffer.at[dst],
                send_sem=sends.at[k],
                recv_sem=recvs.at[k],
                device_id=neighbour(offset),
                device_id_type=MESH,
            )
            copy.start()
            copies.append(copy)
        return copies

    copies = exchange(ext, send_sem, recv_sem)
    row4 = lax.broadcasted_iota(jnp.int32, (4, 128), 0)

    def by_row(values):
        result = jnp.zeros((4, 128), F32)
        for k, value in enumerate(values):
            result = jnp.where(row4 == k, value, result)
        return result

    def shifted(x, y, z):
        cx = (x - 1.5) * EDGE
        cy = (y - 1.5) * EDGE
        cz = (z - 2.5) * EDGE
        return ext[x, y, z] + by_row((cx, cy, cz))

    def norm_of(point):
        square = point * point
        total = square[0:1] + square[1:2] + square[2:3]
        return jnp.where(point[3:4] > 0.5, -0.25 * total, DEAD)

    def expand(x, y, z):
        point = shifted(x, y, z)
        norm = norm_of(point)
        high, low, rest = split3(jnp.where(row4 == 3, norm, point))
        ones = jnp.ones_like(high)
        stack = jnp.concatenate([high, high, high, low, low, rest, ones, jnp.zeros_like(ones)], axis=0)
        moments = jnp.concatenate([high, low, rest, ones], axis=0).astype(BF16)
        mom[x * 4 + y, z] = jnp.concatenate([moments, moments], axis=1)
        return point, norm, stack.T.astype(BF16)

    def pair_columns(k):
        side = lax.rem(k, 2)
        return jnp.where(k < 2, 2 * side, side), jnp.where(k < 2, 2 * side + 1, side + 2)

    def own_column(q):
        return 1 + q // 2, 1 + lax.rem(q, 2)

    def own_step(q, carry):
        x, y = own_column(q)
        for z in range(4):
            point, norm, left = expand(x, y, z + 1)
            lhs[q, z + 1] = left
            blocks = []
            for unit in (LOG2E, 1.0):
                high, low, rest = split3(jnp.where(row4 == 3, unit, (0.5 * unit) * point))
                pieces = by_row(split3(unit * (norm + PEAK)))
                blocks.append(
                    jnp.concatenate(
                        [high, low, rest, high, low, high, pieces, jnp.zeros_like(pieces)], axis=0
                    )
                )
            wts[q * 4 + z] = jnp.concatenate(blocks, axis=1).astype(BF16)
        return carry

    lax.fori_loop(0, 4, own_step, 0)

    def pair_step(k, carry):
        first, second = pair_columns(k)
        for z in range(4):
            one, two = wts[first * 4 + z], wts[second * 4 + z]
            pwts[k * 4 + z] = jnp.concatenate(
                [one[:, 0:128], two[:, 0:128], one[:, 128:256], two[:, 128:256]], axis=1
            )
        return carry

    lax.fori_loop(0, 4, pair_step, 0)

    eye = lax.broadcasted_iota(jnp.int32, (128, 128), 0) == lax.broadcasted_iota(jnp.int32, (128, 128), 1)
    own_pairs = [(iz, jz) for iz in range(4) for jz in range(1, 5) if abs(iz + 1 - jz) <= 1]
    edge_pairs = [(0, 0), (3, 5)]
    all_pairs = [(iz, iz + dz) for iz in range(4) for dz in range(3)]

    def density_tile(left, weight, masked, stores, slot):
        both = jnp.dot(left, weight, preferred_element_type=F32)
        width = both.shape[1] // 2
        fall = jnp.exp2(both[:, 0:width])
        remain = jnp.maximum(both[:, width:], 0.0)
        if masked is not None:
            halves = [remain[:, h * 128 : h * 128 + 128] for h in range(width // 128)]
            halves[masked] = jnp.where(eye, 0.0, halves[masked])
            remain = jnp.concatenate(halves, axis=1)
        part = remain * fall
        rho = part * remain
        mixed = rho + part
        stores[0][slot] = mixed * fall
        stores[1][slot] = mixed + part
        return jnp.sum(rho.reshape(16, 8, width), axis=0)

    def force_tile(j, other, grad, stores, slot):
        if grad.shape[1] == 256:
            other = jnp.concatenate([other, other], axis=1)
        factor = stores[0][slot] + stores[1][slot] * (other + grad)
        high = factor.astype(BF16)
        low = (factor - high.astype(F32)).astype(BF16)
        return jnp.dot(mom[j], jnp.concatenate([high, low], axis=0), preferred_element_type=F32)

    row8 = lax.broadcasted_iota(jnp.int32, (8, 128), 0)

    def grad_column(x, y, inside):
        rows = []
        for z in range(6):
            if z not in inside:
                rows.append(jnp.zeros((8, 128), F32))
                continue
            high, low, rest = split3(GRAD_SCALE * gext[x, y, z])
            rows.append(
                jnp.where(row8 == 0, high, jnp.where(row8 == 1, low, jnp.where(row8 == 2, rest, 0.0)))
            )
        turned = jnp.concatenate(rows, axis=0).T.astype(BF16)
        return jnp.dot(turned, spread[...], preferred_element_type=F32)

    def own_index(column):
        if isinstance(column, int):
            return (column // 4 - 1) * 2 + column % 4 - 1
        return (column // 4 - 1) * 2 + lax.rem(column, 4) - 1

    def own_cells(kind, column):
        if kind == "density":
            return lambda z: lhs[own_index(column), z]
        return lambda z: gwide[own_index(column), :, z * 128 : z * 128 + 128]

    def halo_cells(kind, column):
        x, y = column // 4, lax.rem(column, 4)
        if kind == "density":
            lefts = [expand(x, y, z)[2] for z in range(6)]
            return lambda z: lefts[z]
        wide_grad = grad_column(x, y, range(6))
        return lambda z: wide_grad[:, z * 128 : z * 128 + 128]

    def group(kind, bases, weights, cells, items, stores, slot, first=False):
        totals = {}
        for n, (column, iz, jz, masked) in enumerate(items):
            if kind == "density":
                part = density_tile(cells(column)(jz), weights(iz), masked, stores, slot + n)
            else:
                grad = jnp.concatenate([grow[base + iz] for base in bases], axis=1)
                part = force_tile((column, jz), cells(column)(jz), grad, stores, slot + n)
            totals[iz] = part if iz not in totals else totals[iz] + part
        target = dens if kind == "density" else push
        for iz, total in totals.items():
            for h, base in enumerate(bases):
                block = total[:, h * 128 : h * 128 + 128]
                target[base + iz] = block if first else target[base + iz] + block

    def pair_group(kind, k, cells, items, stores, slot, first=False):
        one, two = pair_columns(k)
        group(kind, [one * 4, two * 4], lambda iz: pwts[k * 4 + iz], cells, items, stores, slot, first)

    def own_part(kind):
        def same_step(k, carry):
            columns = [(1 + k) * 4 + y for y in (1, 2)]
            items = [
                (column, iz, jz, h if jz == iz + 1 else None)
                for h, column in enumerate(columns)
                for iz, jz in own_pairs
            ]
            pair_group(kind, k, lambda c: own_cells(kind, c), items, [own_p, own_r], k * 20, True)
            return carry

        def other_step(p, carry):
            k = p // 2
            column = (2 - k) * 4 + 1 + lax.rem(p, 2)
            items = [(column, iz, jz, None) for iz, jz in own_pairs]
            pair_group(kind, k, lambda c: own_cells(kind, c), items, [own_p, own_r], 40 + p * 10)
            return carry

        lax.fori_loop(0, 2, same_step, 0)
        lax.fori_loop(0, 4, other_step, 0)

    def halo_part(kind):
        def edge_step(k, carry):
            items = [(c, iz, jz, None) for c in (5, 6, 9, 10) for iz, jz in edge_pairs]
            pair_group(kind, k, lambda c: own_cells(kind, c), items, [wide_p, wide_r], k * 8)
            return carry

        def face_step(p, carry):
            k, far = p // 2, lax.rem(p, 2)
            side = 1 + lax.rem(k, 2)
            near = k < 2
            column = jnp.where(near, 4 * (3 * (side - 1)) + 1 + far, 4 * (1 + far) + 3 * (side - 1))
            items = [(column, iz, jz, None) for iz, jz in all_pairs]
            cells = halo_cells(kind, column)
            pair_group(kind, k, lambda c: cells, items, [wide_p, wide_r], 16 + p * 12)
            return carry

        def corner_step(q, carry):
            column = 12 * (q // 2) + 3 * lax.rem(q, 2)
            cells = halo_cells(kind, column)
            group(
                kind, [q * 4], lambda iz: wts[q * 4 + iz], lambda c: cells,
                [(column, iz, jz, None) for iz, jz in all_pairs], [single_p, single_r], q * 12,
            )
            return carry

        lax.fori_loop(0, 2, edge_step, 0)
        lax.fori_loop(0, 8, face_step, 0)
        lax.fori_loop(0, 4, corner_step, 0)

    own_part("density")

    for copy in copies:
        copy.wait()

    def edge_expand(x, carry):
        for y in (1, 2):
            for z in (0, 5):
                lhs[2 * x + y - 1, z] = expand(x + 1, y, z)[2]
        return carry

    lax.fori_loop(0, 2, edge_expand, 0)

    halo_part("density")

    def grad_step(q, carry):
        x, y = own_column(q)
        for z in range(4):
            density = RHO_SCALE * jnp.sum(dens[q * 4 + z], axis=0, keepdims=True)
            gext[x, y, z + 1] = ext[x, y, z + 1, 3:4, :] * 2.0 * (density - 1.0)
        return carry

    lax.fori_loop(0, 4, grad_step, 0)
    copies = exchange(gext, gsend_sem, grecv_sem)

    spread_row = lax.broadcasted_iota(jnp.int32, (GRAD_ROWS, 768), 0) // 8
    spread_lane = lax.broadcasted_iota(jnp.int32, (GRAD_ROWS, 768), 1) // 128
    spread[...] = jnp.where(spread_row == spread_lane, 1.0, 0.0).astype(BF16)

    for q in range(4):
        for z in range(4):
            grow[q * 4 + z] = GRAD_SCALE * gext[1 + q // 2, 1 + q % 2, z + 1]
        gwide[q] = grad_column(1 + q // 2, 1 + q % 2, range(1, 5))

    own_part("force")

    for copy in copies:
        copy.wait()

    for q in range(4):
        edges = grad_column(1 + q // 2, 1 + q % 2, (0, 5))
        gwide[q, :, 0:128] = edges[:, 0:128]
        gwide[q, :, 640:768] = edges[:, 640:768]

    halo_part("force")

    def finish(q, carry):
        x, y = own_column(q)
        for z in range(4):
            total = push[q * 4 + z]
            point = shifted(x, y, z + 1)
            live = point[3:4]
            force = FORCE_SCALE * (total[0:4] + total[4:8] + total[8:12] - point * total[12:13])
            for c in range(3):
                place = pos_ref[c, x - 1, y - 1, z : z + 1, :]
                velocity = vel_ref[c, x - 1, y - 1, z : z + 1, :] + TIME_STEP * force[c : c + 1]
                vout_ref[c, x - 1, y - 1, z : z + 1, :] = velocity * live
                mout_ref[c, x - 1, y - 1, z : z + 1, :] = (
                    (place + TIME_STEP * velocity) - place
                ) * live
        return carry

    lax.fori_loop(0, 4, finish, 0)


def body(positions, velocities, counts):
    vmem = pl.BlockSpec(memory_space=pltpu.VMEM)
    hbm = pl.BlockSpec(memory_space=pltpu.HBM)
    shape = jax.ShapeDtypeStruct(positions.shape, F32)
    links = len(OFFSETS)
    return pl.pallas_call(
        kernel,
        out_shape=(shape, shape),
        in_specs=[hbm, hbm, hbm],
        out_specs=(vmem, vmem),
        scratch_shapes=[
            pltpu.VMEM(positions.shape, F32),
            pltpu.VMEM(positions.shape, F32),
            pltpu.SMEM(counts.shape, jnp.int32),
            pltpu.VMEM(EXT + (4, 128), F32),
            pltpu.VMEM(EXT + (1, 128), F32),
            pltpu.VMEM((4, 6, 128, 32), BF16),
            pltpu.VMEM((COLUMNS, 6, 16, 256), BF16),
            pltpu.VMEM((CELLS, 32, 256), BF16),
            pltpu.VMEM((CELLS, 32, 512), BF16),
            pltpu.VMEM((4, 128, 768), F32),
            pltpu.VMEM((CELLS, 1, 128), F32),
            pltpu.VMEM((GRAD_ROWS, 768), BF16),
            pltpu.VMEM((80, 128, 256), F32),
            pltpu.VMEM((80, 128, 256), F32),
            pltpu.VMEM((112, 128, 256), F32),
            pltpu.VMEM((112, 128, 256), F32),
            pltpu.VMEM((48, 128, 128), F32),
            pltpu.VMEM((48, 128, 128), F32),
            pltpu.VMEM((CELLS, 8, 128), F32),
            pltpu.VMEM((CELLS, 16, 128), F32),
            pltpu.SemaphoreType.DMA((3,)),
            pltpu.SemaphoreType.DMA((links,)),
            pltpu.SemaphoreType.DMA((links,)),
            pltpu.SemaphoreType.DMA((links,)),
            pltpu.SemaphoreType.DMA((links,)),
        ],
        compiler_params=pltpu.CompilerParams(
            collective_id=0, has_side_effects=True, vmem_limit_bytes=62 * 1024 * 1024
        ),
    )(positions, velocities, counts)


def solution(mesh):
    spec = P(None, "gx", "gy", "gz", None)
    return jax.shard_map(
        body,
        mesh=mesh,
        in_specs=(spec, spec, P("gx", "gy", "gz")),
        out_specs=(spec, spec),
        check_vma=False,
    )
```

```python
import functools
import math

import jax
import jax.numpy as jnp
from jax import lax
from jax.experimental import pallas as pl
from jax.experimental.pallas import tpu as pltpu
from jax.sharding import PartitionSpec as P

MESH = pl.DeviceIdType.MESH
EDGE = 11.0
LOG2E = math.log2(math.e)
PEAK = 25.0 / 4.0
DEAD = -30000.0
RHO_SCALE = 0.4 * math.exp(-PEAK) / PEAK**2
FORCE_SCALE = 2.0 * -0.15 * math.exp(-2.0 * PEAK) / PEAK**2
GRAD_SCALE = 2.0 / 3.0 * math.exp(PEAK)
TIME_STEP = 0.5
OFFSETS = [
    (dx, dy, dz)
    for dx in (-1, 0, 1)
    for dy in (-1, 0, 1)
    for dz in (-1, 0, 1)
    if (dx, dy, dz) != (0, 0, 0)
]
OWN = (2, 2, 4)
EXT = (4, 4, 6)
CELLS = OWN[0] * OWN[1] * OWN[2]
COLUMNS = EXT[0] * EXT[1]
GRAD_ROWS = 8 * EXT[2]
F32, BF16 = jnp.float32, jnp.bfloat16


def source_slice(step, size):
    if step == 0:
        return pl.ds(1, size)
    return pl.ds(size if step > 0 else 1, 1)


def target_slice(step, size):
    if step == 0:
        return pl.ds(1, size)
    return pl.ds(0 if step > 0 else size + 1, 1)


def round16(value):
    return value.astype(BF16).astype(F32)


def split3(value):
    high = round16(value)
    rest = value - high
    low = round16(rest)
    return high, low, rest - low


def kernel(
    pos_hbm, vel_hbm, cnt_hbm, vout_ref, mout_ref,
    pos_ref, vel_ref, cnt_ref, ext, gext, lhs, mom, wts, pwts, gwide, grow, spread, own_p, own_r, wide_p, wide_r, single_p, single_r, dens, push,
    load_sem, send_sem, recv_sem, gsend_sem, grecv_sem,
):
    loads = [
        pltpu.make_async_copy(source, target, load_sem.at[k])
        for k, (source, target) in enumerate(
            ((pos_hbm, pos_ref), (cnt_hbm, cnt_ref), (vel_hbm, vel_ref))
        )
    ]
    for load in loads:
        load.start()

    sizes = [lax.axis_size(name) for name in ("gx", "gy", "gz")]
    me = [lax.axis_index(name) for name in ("gx", "gy", "gz")]

    def neighbour(offset):
        return tuple(lax.rem(m + d + n, n) for m, d, n in zip(me, offset, sizes))

    barrier = pltpu.get_barrier_semaphore()
    for offset in OFFSETS:
        pl.semaphore_signal(barrier, inc=1, device_id=neighbour(offset), device_id_type=MESH)

    for load in loads:
        load.wait()
    lane = lax.broadcasted_iota(jnp.int32, (1, 128), 1)
    for x in range(OWN[0]):
        for y in range(OWN[1]):
            for z in range(OWN[2]):
                for c in range(3):
                    ext[1 + x, 1 + y, 1 + z, c : c + 1, :] = (
                        pos_ref[c, x, y, z : z + 1, :] - 0.5 * EDGE
                    )
                live = jnp.where(lane < cnt_ref[x, y, z], 1.0, 0.0)
                ext[1 + x, 1 + y, 1 + z, 3:4, :] = live

    pl.semaphore_wait(barrier, len(OFFSETS))

    def exchange(buffer, sends, recvs):
        copies = []
        for k, offset in enumerate(OFFSETS):
            src = tuple(source_slice(d, n) for d, n in zip(offset, OWN))
            dst = tuple(target_slice(d, n) for d, n in zip(offset, OWN))
            copy = pltpu.make_async_remote_copy(
                src_ref=buffer.at[src],
                dst_ref=buffer.at[dst],
                send_sem=sends.at[k],
                recv_sem=recvs.at[k],
                device_id=neighbour(offset),
                device_id_type=MESH,
            )
            copy.start()
            copies.append(copy)
        return copies

    copies = exchange(ext, send_sem, recv_sem)
    row4 = lax.broadcasted_iota(jnp.int32, (4, 128), 0)

    def by_row(values):
        result = jnp.zeros((4, 128), F32)
        for k, value in enumerate(values):
            result = jnp.where(row4 == k, value, result)
        return result

    def shifted(x, y, z):
        cx = (x - 1.5) * EDGE
        cy = (y - 1.5) * EDGE
        cz = (z - 2.5) * EDGE
        return ext[x, y, z] + by_row((cx, cy, cz))

    def norm_of(point):
        square = point * point
        total = square[0:1] + square[1:2] + square[2:3]
        return jnp.where(point[3:4] > 0.5, -0.25 * total, DEAD)

    def expand(x, y, z):
        point = shifted(x, y, z)
        norm = norm_of(point)
        high, low, rest = split3(jnp.where(row4 == 3, norm, point))
        ones = jnp.ones_like(high)
        stack = jnp.concatenate([high, high, high, low, low, rest, ones, jnp.zeros_like(ones)], axis=0)
        moments = jnp.concatenate([high, low, rest, ones], axis=0).astype(BF16)
        mom[x * 4 + y, z] = jnp.concatenate([moments, moments], axis=1)
        return point, norm, stack.T.astype(BF16)

    def pair_columns(k):
        side = lax.rem(k, 2)
        return jnp.where(k < 2, 2 * side, side), jnp.where(k < 2, 2 * side + 1, side + 2)

    def own_column(q):
        return 1 + q // 2, 1 + lax.rem(q, 2)

    def own_step(q, carry):
        x, y = own_column(q)
        for z in range(4):
            point, norm, left = expand(x, y, z + 1)
            lhs[q, z + 1] = left
            blocks = []
            for unit in (LOG2E, 1.0):
                high, low, rest = split3(jnp.where(row4 == 3, unit, (0.5 * unit) * point))
                pieces = by_row(split3(unit * (norm + PEAK)))
                blocks.append(
                    jnp.concatenate(
                        [high, low, rest, high, low, high, pieces, jnp.zeros_like(pieces)], axis=0
                    )
                )
            wts[q * 4 + z] = jnp.concatenate(blocks, axis=1).astype(BF16)
        return carry

    lax.fori_loop(0, 4, own_step, 0)

    def pair_step(k, carry):
        first, second = pair_columns(k)
        for z in range(4):
            one, two = wts[first * 4 + z], wts[second * 4 + z]
            pwts[k * 4 + z] = jnp.concatenate(
                [one[:, 0:128], two[:, 0:128], one[:, 128:256], two[:, 128:256]], axis=1
            )
        return carry

    lax.fori_loop(0, 4, pair_step, 0)

    eye = lax.broadcasted_iota(jnp.int32, (128, 128), 0) == lax.broadcasted_iota(jnp.int32, (128, 128), 1)
    own_pairs = [(iz, jz) for iz in range(4) for jz in range(1, 5) if abs(iz + 1 - jz) <= 1]
    edge_pairs = [(0, 0), (3, 5)]
    all_pairs = [(iz, iz + dz) for iz in range(4) for dz in range(3)]

    def density_tile(left, weight, masked, stores, slot):
        both = jnp.dot(left, weight, preferred_element_type=F32)
        width = both.shape[1] // 2
        fall = jnp.exp2(both[:, 0:width])
        remain = jnp.maximum(both[:, width:], 0.0)
        if masked is not None:
            halves = [remain[:, h * 128 : h * 128 + 128] for h in range(width // 128)]
            halves[masked] = jnp.where(eye, 0.0, halves[masked])
            remain = jnp.concatenate(halves, axis=1)
        part = remain * fall
        rho = part * remain
        mixed = rho + part
        stores[0][slot] = mixed * fall
        stores[1][slot] = mixed + part
        return jnp.sum(rho.reshape(16, 8, width), axis=0)

    def force_tile(j, other, grad, stores, slot):
        if grad.shape[1] == 256:
            other = jnp.concatenate([other, other], axis=1)
        factor = stores[0][slot] + stores[1][slot] * (other + grad)
        high = factor.astype(BF16)
        low = (factor - high.astype(F32)).astype(BF16)
        return jnp.dot(mom[j], jnp.concatenate([high, low], axis=0), preferred_element_type=F32)

    row8 = lax.broadcasted_iota(jnp.int32, (8, 128), 0)

    def grad_column(x, y, inside):
        rows = []
        for z in range(6):
            if z not in inside:
                rows.append(jnp.zeros((8, 128), F32))
                continue
            high, low, rest = split3(GRAD_SCALE * gext[x, y, z])
            rows.append(
                jnp.where(row8 == 0, high, jnp.where(row8 == 1, low, jnp.where(row8 == 2, rest, 0.0)))
            )
        turned = jnp.concatenate(rows, axis=0).T.astype(BF16)
        return jnp.dot(turned, spread[...], preferred_element_type=F32)

    def own_index(column):
        if isinstance(column, int):
            return (column // 4 - 1) * 2 + column % 4 - 1
        return (column // 4 - 1) * 2 + lax.rem(column, 4) - 1

    def own_cells(kind, column):
        if kind == "density":
            return lambda z: lhs[own_index(column), z]
        return lambda z: gwide[own_index(column), :, z * 128 : z * 128 + 128]

    def halo_cells(kind, column):
        x, y = column // 4, lax.rem(column, 4)
        if kind == "density":
            lefts = [expand(x, y, z)[2] for z in range(6)]
            return lambda z: lefts[z]
        wide_grad = grad_column(x, y, range(6))
        return lambda z: wide_grad[:, z * 128 : z * 128 + 128]

    def group(kind, bases, weights, cells, items, stores, slot, first=False):
        totals = {}
        for n, (column, iz, jz, masked, *place) in enumerate(items):
            if kind == "density":
                part = density_tile(cells(column)(jz), weights(iz), masked, stores, slot + n)
            else:
                grad = jnp.concatenate([grow[base + iz] for base in bases], axis=1)
                part = force_tile(((place or [column])[0], jz), cells(column)(jz), grad, stores, slot + n)
            totals[iz] = part if iz not in totals else totals[iz] + part
        target = dens if kind == "density" else push
        for iz, total in totals.items():
            for h, base in enumerate(bases):
                block = total[:, h * 128 : h * 128 + 128]
                target[base + iz] = block if first else target[base + iz] + block

    def pair_group(kind, k, cells, items, stores, slot, first=False):
        one, two = pair_columns(k)
        group(kind, [one * 4, two * 4], lambda iz: pwts[k * 4 + iz], cells, items, stores, slot, first)

    def own_part(kind):
        def same_step(k, carry):
            columns = [(1 + k) * 4 + y for y in (1, 2)]
            items = [
                (column, iz, jz, h if jz == iz + 1 else None)
                for h, column in enumerate(columns)
                for iz, jz in own_pairs
            ]
            pair_group(kind, k, lambda c: own_cells(kind, c), items, [own_p, own_r], k * 20, True)
            return carry

        def other_step(p, carry):
            k = p // 2
            column = (2 - k) * 4 + 1 + lax.rem(p, 2)
            items = [(column, iz, jz, None) for iz, jz in own_pairs]
            pair_group(kind, k, lambda c: own_cells(kind, c), items, [own_p, own_r], 40 + p * 10)
            return carry

        lax.fori_loop(0, 2, same_step, 0)
        lax.fori_loop(0, 4, other_step, 0)

    def halo_part(kind):
        def edge_step(k, carry):
            items = [(c, iz, jz, None) for c in (5, 6, 9, 10) for iz, jz in edge_pairs]
            pair_group(kind, k, lambda c: own_cells(kind, c), items, [wide_p, wide_r], k * 8)
            return carry

        def face_step(k, carry):
            side = 1 + lax.rem(k, 2)
            near = k < 2
            cells, items = {}, []
            for far in range(2):
                column = jnp.where(
                    near, 4 * (3 * (side - 1)) + 1 + far, 4 * (1 + far) + 3 * (side - 1)
                )
                cells[far] = halo_cells(kind, column)
                items += [(far, iz, jz, None, column) for iz, jz in all_pairs]
            pair_group(kind, k, lambda c: cells[c], items, [wide_p, wide_r], 16 + k * 24)
            return carry

        def corner_step(q_x, carry):
            for q_y in range(2):
                q = q_x * 2 + q_y
                column = 12 * q_x + 3 * q_y
                cells = halo_cells(kind, column)
                group(
                    kind, [q * 4], lambda iz: wts[q * 4 + iz], lambda c: cells,
                    [(column, iz, jz, None) for iz, jz in all_pairs], [single_p, single_r], q * 12,
                )
            return carry

        lax.fori_loop(0, 2, edge_step, 0)
        lax.fori_loop(0, 4, face_step, 0)
        lax.fori_loop(0, 2, corner_step, 0)

    own_part("density")

    for copy in copies:
        copy.wait()

    def edge_expand(x, carry):
        for y in (1, 2):
            for z in (0, 5):
                lhs[2 * x + y - 1, z] = expand(x + 1, y, z)[2]
        return carry

    lax.fori_loop(0, 2, edge_expand, 0)

    halo_part("density")

    def grad_step(q, carry):
        x, y = own_column(q)
        for z in range(4):
            density = RHO_SCALE * jnp.sum(dens[q * 4 + z], axis=0, keepdims=True)
            gext[x, y, z + 1] = ext[x, y, z + 1, 3:4, :] * 2.0 * (density - 1.0)
        return carry

    lax.fori_loop(0, 4, grad_step, 0)
    copies = exchange(gext, gsend_sem, grecv_sem)

    spread_row = lax.broadcasted_iota(jnp.int32, (GRAD_ROWS, 768), 0) // 8
    spread_lane = lax.broadcasted_iota(jnp.int32, (GRAD_ROWS, 768), 1) // 128
    spread[...] = jnp.where(spread_row == spread_lane, 1.0, 0.0).astype(BF16)

    for q in range(4):
        for z in range(4):
            grow[q * 4 + z] = GRAD_SCALE * gext[1 + q // 2, 1 + q % 2, z + 1]
        gwide[q] = grad_column(1 + q // 2, 1 + q % 2, range(1, 5))

    own_part("force")

    for copy in copies:
        copy.wait()

    for q in range(4):
        edges = grad_column(1 + q // 2, 1 + q % 2, (0, 5))
        gwide[q, :, 0:128] = edges[:, 0:128]
        gwide[q, :, 640:768] = edges[:, 640:768]

    halo_part("force")

    def finish(q, carry):
        x, y = own_column(q)
        for z in range(4):
            total = push[q * 4 + z]
            point = shifted(x, y, z + 1)
            live = point[3:4]
            force = FORCE_SCALE * (total[0:4] + total[4:8] + total[8:12] - point * total[12:13])
            for c in range(3):
                place = pos_ref[c, x - 1, y - 1, z : z + 1, :]
                velocity = vel_ref[c, x - 1, y - 1, z : z + 1, :] + TIME_STEP * force[c : c + 1]
                vout_ref[c, x - 1, y - 1, z : z + 1, :] = velocity * live
                mout_ref[c, x - 1, y - 1, z : z + 1, :] = (
                    (place + TIME_STEP * velocity) - place
                ) * live
        return carry

    lax.fori_loop(0, 4, finish, 0)


def body(positions, velocities, counts):
    vmem = pl.BlockSpec(memory_space=pltpu.VMEM)
    hbm = pl.BlockSpec(memory_space=pltpu.HBM)
    shape = jax.ShapeDtypeStruct(positions.shape, F32)
    links = len(OFFSETS)
    return pl.pallas_call(
        kernel,
        out_shape=(shape, shape),
        in_specs=[hbm, hbm, hbm],
        out_specs=(vmem, vmem),
        scratch_shapes=[
            pltpu.VMEM(positions.shape, F32),
            pltpu.VMEM(positions.shape, F32),
            pltpu.SMEM(counts.shape, jnp.int32),
            pltpu.VMEM(EXT + (4, 128), F32),
            pltpu.VMEM(EXT + (1, 128), F32),
            pltpu.VMEM((4, 6, 128, 32), BF16),
            pltpu.VMEM((COLUMNS, 6, 16, 256), BF16),
            pltpu.VMEM((CELLS, 32, 256), BF16),
            pltpu.VMEM((CELLS, 32, 512), BF16),
            pltpu.VMEM((4, 128, 768), F32),
            pltpu.VMEM((CELLS, 1, 128), F32),
            pltpu.VMEM((GRAD_ROWS, 768), BF16),
            pltpu.VMEM((80, 128, 256), F32),
            pltpu.VMEM((80, 128, 256), F32),
            pltpu.VMEM((112, 128, 256), F32),
            pltpu.VMEM((112, 128, 256), F32),
            pltpu.VMEM((48, 128, 128), F32),
            pltpu.VMEM((48, 128, 128), F32),
            pltpu.VMEM((CELLS, 8, 128), F32),
            pltpu.VMEM((CELLS, 16, 128), F32),
            pltpu.SemaphoreType.DMA((3,)),
            pltpu.SemaphoreType.DMA((links,)),
            pltpu.SemaphoreType.DMA((links,)),
            pltpu.SemaphoreType.DMA((links,)),
            pltpu.SemaphoreType.DMA((links,)),
        ],
        compiler_params=pltpu.CompilerParams(
            collective_id=0, has_side_effects=True, vmem_limit_bytes=62 * 1024 * 1024
        ),
    )(positions, velocities, counts)


def solution(mesh):
    spec = P(None, "gx", "gy", "gz", None)
    return jax.shard_map(
        body,
        mesh=mesh,
        in_specs=(spec, spec, P("gx", "gy", "gz")),
        out_specs=(spec, spec),
        check_vma=False,
    )
```

```python
import functools
import math

import jax
import jax.numpy as jnp
from jax import lax
from jax.experimental import pallas as pl
from jax.experimental.pallas import tpu as pltpu
from jax.sharding import PartitionSpec as P

MESH = pl.DeviceIdType.MESH
EDGE = 11.0
LOG2E = math.log2(math.e)
PEAK = 25.0 / 4.0
DEAD = -30000.0
RHO_SCALE = 0.4 * math.exp(-PEAK) / PEAK**2
FORCE_SCALE = 2.0 * -0.15 * math.exp(-2.0 * PEAK) / PEAK**2
GRAD_SCALE = 2.0 / 3.0 * math.exp(PEAK)
TIME_STEP = 0.5
OFFSETS = [
    (dx, dy, dz)
    for dx in (-1, 0, 1)
    for dy in (-1, 0, 1)
    for dz in (-1, 0, 1)
    if (dx, dy, dz) != (0, 0, 0)
]
OWN = (2, 2, 4)
EXT = (4, 4, 6)
CELLS = OWN[0] * OWN[1] * OWN[2]
COLUMNS = EXT[0] * EXT[1]
GRAD_ROWS = 8 * EXT[2]
F32, BF16 = jnp.float32, jnp.bfloat16


def source_slice(step, size):
    if step == 0:
        return pl.ds(1, size)
    return pl.ds(size if step > 0 else 1, 1)


def target_slice(step, size):
    if step == 0:
        return pl.ds(1, size)
    return pl.ds(0 if step > 0 else size + 1, 1)


def round16(value):
    return value.astype(BF16).astype(F32)


def split3(value):
    high = round16(value)
    rest = value - high
    low = round16(rest)
    return high, low, rest - low


def kernel(
    pos_hbm, vel_hbm, cnt_hbm, vout_ref, mout_ref,
    pos_ref, vel_ref, cnt_ref, ext, gext, lhs, mom, wts, pwts, gwide, grow, spread, own_p, own_r, wide_p, wide_r, single_p, single_r, dens, push,
    load_sem, send_sem, recv_sem, gsend_sem, grecv_sem,
):
    loads = [
        pltpu.make_async_copy(source, target, load_sem.at[k])
        for k, (source, target) in enumerate(
            ((pos_hbm, pos_ref), (cnt_hbm, cnt_ref), (vel_hbm, vel_ref))
        )
    ]
    for load in loads:
        load.start()

    sizes = [lax.axis_size(name) for name in ("gx", "gy", "gz")]
    me = [lax.axis_index(name) for name in ("gx", "gy", "gz")]

    def neighbour(offset):
        return tuple(lax.rem(m + d + n, n) for m, d, n in zip(me, offset, sizes))

    barrier = pltpu.get_barrier_semaphore()
    for offset in OFFSETS:
        pl.semaphore_signal(barrier, inc=1, device_id=neighbour(offset), device_id_type=MESH)

    for load in loads:
        load.wait()
    lane = lax.broadcasted_iota(jnp.int32, (1, 128), 1)
    for x in range(OWN[0]):
        for y in range(OWN[1]):
            for z in range(OWN[2]):
                for c in range(3):
                    ext[1 + x, 1 + y, 1 + z, c : c + 1, :] = (
                        pos_ref[c, x, y, z : z + 1, :] - 0.5 * EDGE
                    )
                live = jnp.where(lane < cnt_ref[x, y, z], 1.0, 0.0)
                ext[1 + x, 1 + y, 1 + z, 3:4, :] = live

    pl.semaphore_wait(barrier, len(OFFSETS))

    def exchange(buffer, sends, recvs):
        copies = []
        for k, offset in enumerate(OFFSETS):
            src = tuple(source_slice(d, n) for d, n in zip(offset, OWN))
            dst = tuple(target_slice(d, n) for d, n in zip(offset, OWN))
            copy = pltpu.make_async_remote_copy(
                src_ref=buffer.at[src],
                dst_ref=buffer.at[dst],
                send_sem=sends.at[k],
                recv_sem=recvs.at[k],
                device_id=neighbour(offset),
                device_id_type=MESH,
            )
            copy.start()
            copies.append(copy)
        return copies

    copies = exchange(ext, send_sem, recv_sem)
    row4 = lax.broadcasted_iota(jnp.int32, (4, 128), 0)

    def by_row(values):
        result = jnp.zeros((4, 128), F32)
        for k, value in enumerate(values):
            result = jnp.where(row4 == k, value, result)
        return result

    def shifted(x, y, z):
        cx = (x - 1.5) * EDGE
        cy = (y - 1.5) * EDGE
        cz = (z - 2.5) * EDGE
        return ext[x, y, z] + by_row((cx, cy, cz))

    def norm_of(point):
        square = point * point
        total = square[0:1] + square[1:2] + square[2:3]
        return jnp.where(point[3:4] > 0.5, -0.25 * total, DEAD)

    def expand(x, y, z):
        point = shifted(x, y, z)
        norm = norm_of(point)
        high, low, rest = split3(jnp.where(row4 == 3, norm, point))
        ones = jnp.ones_like(high)
        stack = jnp.concatenate([high, high, high, low, low, rest, ones, jnp.zeros_like(ones)], axis=0)
        moments = jnp.concatenate([high, low, rest, ones], axis=0).astype(BF16)
        mom[x * 4 + y, z] = jnp.concatenate([moments, moments], axis=1)
        return point, norm, stack.T.astype(BF16)

    def pair_columns(k):
        side = lax.rem(k, 2)
        return jnp.where(k < 2, 2 * side, side), jnp.where(k < 2, 2 * side + 1, side + 2)

    def own_column(q):
        return 1 + q // 2, 1 + lax.rem(q, 2)

    def own_step(q, carry):
        x, y = own_column(q)
        for z in range(4):
            point, norm, left = expand(x, y, z + 1)
            lhs[q, z + 1] = left
            blocks = []
            for unit in (LOG2E, 1.0):
                high, low, rest = split3(jnp.where(row4 == 3, unit, (0.5 * unit) * point))
                pieces = by_row(split3(unit * (norm + PEAK)))
                blocks.append(
                    jnp.concatenate(
                        [high, low, rest, high, low, high, pieces, jnp.zeros_like(pieces)], axis=0
                    )
                )
            wts[q * 4 + z] = jnp.concatenate(blocks, axis=1).astype(BF16)
        return carry

    lax.fori_loop(0, 4, own_step, 0)

    def pair_step(k, carry):
        first, second = pair_columns(k)
        for z in range(4):
            one, two = wts[first * 4 + z], wts[second * 4 + z]
            pwts[k * 4 + z] = jnp.concatenate(
                [one[:, 0:128], two[:, 0:128], one[:, 128:256], two[:, 128:256]], axis=1
            )
        return carry

    lax.fori_loop(0, 4, pair_step, 0)

    eye = lax.broadcasted_iota(jnp.int32, (128, 128), 0) == lax.broadcasted_iota(jnp.int32, (128, 128), 1)
    own_pairs = [(iz, jz) for iz in range(4) for jz in range(1, 5) if abs(iz + 1 - jz) <= 1]
    edge_pairs = [(0, 0), (3, 5)]
    all_pairs = [(iz, iz + dz) for iz in range(4) for dz in range(3)]

    def density_tile(left, weight, masked, stores, slot):
        both = jnp.dot(left, weight, preferred_element_type=F32)
        width = both.shape[1] // 2
        fall = jnp.exp2(both[:, 0:width])
        remain = jnp.maximum(both[:, width:], 0.0)
        if masked is not None:
            halves = [remain[:, h * 128 : h * 128 + 128] for h in range(width // 128)]
            halves[masked] = jnp.where(eye, 0.0, halves[masked])
            remain = jnp.concatenate(halves, axis=1)
        part = remain * fall
        rho = part * remain
        mixed = rho + part
        stores[0][slot] = mixed * fall
        stores[1][slot] = mixed + part
        return jnp.sum(rho.reshape(16, 8, width), axis=0)

    def force_tile(j, other, grad, stores, slot):
        if grad.shape[1] == 256:
            other = jnp.concatenate([other, other], axis=1)
        factor = stores[0][slot] + stores[1][slot] * (other + grad)
        high = factor.astype(BF16)
        low = (factor - high.astype(F32)).astype(BF16)
        return jnp.dot(mom[j], jnp.concatenate([high, low], axis=0), preferred_element_type=F32)

    row8 = lax.broadcasted_iota(jnp.int32, (8, 128), 0)

    def grad_column(x, y, inside):
        rows = []
        for z in range(6):
            if z not in inside:
                rows.append(jnp.zeros((8, 128), F32))
                continue
            high, low, rest = split3(GRAD_SCALE * gext[x, y, z])
            rows.append(
                jnp.where(row8 == 0, high, jnp.where(row8 == 1, low, jnp.where(row8 == 2, rest, 0.0)))
            )
        turned = jnp.concatenate(rows, axis=0).T.astype(BF16)
        return jnp.dot(turned, spread[...], preferred_element_type=F32)

    def own_index(column):
        if isinstance(column, int):
            return (column // 4 - 1) * 2 + column % 4 - 1
        return (column // 4 - 1) * 2 + lax.rem(column, 4) - 1

    def own_cells(kind, column):
        if kind == "density":
            return lambda z: lhs[own_index(column), z]
        return lambda z: gwide[own_index(column), :, z * 128 : z * 128 + 128]

    def halo_cells(kind, column):
        x, y = column // 4, lax.rem(column, 4)
        if kind == "density":
            lefts = [expand(x, y, z)[2] for z in range(6)]
            return lambda z: lefts[z]
        wide_grad = grad_column(x, y, range(6))
        return lambda z: wide_grad[:, z * 128 : z * 128 + 128]

    def group(kind, bases, weights, cells, items, stores, slot, first=False):
        totals = {}
        for n, (column, iz, jz, masked, *place) in enumerate(items):
            if kind == "density":
                part = density_tile(cells(column)(jz), weights(iz), masked, stores, slot + n)
            else:
                grad = jnp.concatenate([grow[base + iz] for base in bases], axis=1)
                part = force_tile(((place or [column])[0], jz), cells(column)(jz), grad, stores, slot + n)
            totals[iz] = part if iz not in totals else totals[iz] + part
        target = dens if kind == "density" else push
        for iz, total in totals.items():
            for h, base in enumerate(bases):
                block = total[:, h * 128 : h * 128 + 128]
                target[base + iz] = block if first else target[base + iz] + block

    def pair_group(kind, k, cells, items, stores, slot, first=False):
        one, two = pair_columns(k)
        group(kind, [one * 4, two * 4], lambda iz: pwts[k * 4 + iz], cells, items, stores, slot, first)

    def own_part(kind):
        def same_step(k, carry):
            columns = [(1 + k) * 4 + y for y in (1, 2)]
            items = [
                (column, iz, jz, h if jz == iz + 1 else None)
                for h, column in enumerate(columns)
                for iz, jz in own_pairs
            ]
            pair_group(kind, k, lambda c: own_cells(kind, c), items, [own_p, own_r], k * 20, True)
            return carry

        def other_step(p, carry):
            k = p // 2
            column = (2 - k) * 4 + 1 + lax.rem(p, 2)
            items = [(column, iz, jz, None) for iz, jz in own_pairs]
            pair_group(kind, k, lambda c: own_cells(kind, c), items, [own_p, own_r], 40 + p * 10)
            return carry

        lax.fori_loop(0, 2, same_step, 0)
        lax.fori_loop(0, 4, other_step, 0)

    def halo_part(kind):
        def edge_step(k, carry):
            items = [(c, iz, jz, None) for c in (5, 6, 9, 10) for iz, jz in edge_pairs]
            pair_group(kind, k, lambda c: own_cells(kind, c), items, [wide_p, wide_r], k * 8)
            return carry

        def face_step(k, carry):
            side = 1 + lax.rem(k, 2)
            near = k < 2
            cells, items = {}, []
            for far in range(2):
                column = jnp.where(
                    near, 4 * (3 * (side - 1)) + 1 + far, 4 * (1 + far) + 3 * (side - 1)
                )
                cells[far] = halo_cells(kind, column)
                items += [(far, iz, jz, None, column) for iz, jz in all_pairs]
            corner = 12 * (k // 2) + 3 * side - 3
            corner_cells = halo_cells(kind, corner)
            pair_group(kind, k, lambda c: cells[c], items, [wide_p, wide_r], 16 + k * 24)
            group(
                kind, [k * 4], lambda iz: wts[k * 4 + iz], lambda c: corner_cells,
                [(corner, iz, jz, None) for iz, jz in all_pairs], [single_p, single_r], k * 12,
            )
            return carry

        lax.fori_loop(0, 2, edge_step, 0)
        lax.fori_loop(0, 4, face_step, 0)

    own_part("density")

    for copy in copies:
        copy.wait()

    for q in range(4):
        for z in (0, 5):
            lhs[q, z] = expand(1 + q // 2, 1 + q % 2, z)[2]

    halo_part("density")

    for q in range(4):
        x, y = 1 + q // 2, 1 + q % 2
        for z in range(4):
            density = RHO_SCALE * jnp.sum(dens[q * 4 + z], axis=0, keepdims=True)
            gext[x, y, z + 1] = ext[x, y, z + 1, 3:4, :] * 2.0 * (density - 1.0)

    copies = exchange(gext, gsend_sem, grecv_sem)

    spread_row = lax.broadcasted_iota(jnp.int32, (GRAD_ROWS, 768), 0) // 8
    spread_lane = lax.broadcasted_iota(jnp.int32, (GRAD_ROWS, 768), 1) // 128
    spread[...] = jnp.where(spread_row == spread_lane, 1.0, 0.0).astype(BF16)

    for q in range(4):
        for z in range(4):
            grow[q * 4 + z] = GRAD_SCALE * gext[1 + q // 2, 1 + q % 2, z + 1]
        gwide[q] = grad_column(1 + q // 2, 1 + q % 2, range(1, 5))

    own_part("force")

    for copy in copies:
        copy.wait()

    for q in range(4):
        edges = grad_column(1 + q // 2, 1 + q % 2, (0, 5))
        gwide[q, :, 0:128] = edges[:, 0:128]
        gwide[q, :, 640:768] = edges[:, 640:768]

    halo_part("force")

    for q in range(4):
        x, y = 1 + q // 2, 1 + q % 2
        for z in range(4):
            total = push[q * 4 + z]
            point = shifted(x, y, z + 1)
            live = point[3:4]
            force = FORCE_SCALE * (total[0:4] + total[4:8] + total[8:12] - point * total[12:13])
            for c in range(3):
                place = pos_ref[c, x - 1, y - 1, z : z + 1, :]
                velocity = vel_ref[c, x - 1, y - 1, z : z + 1, :] + TIME_STEP * force[c : c + 1]
                vout_ref[c, x - 1, y - 1, z : z + 1, :] = velocity * live
                mout_ref[c, x - 1, y - 1, z : z + 1, :] = (
                    (place + TIME_STEP * velocity) - place
                ) * live


def body(positions, velocities, counts):
    vmem = pl.BlockSpec(memory_space=pltpu.VMEM)
    hbm = pl.BlockSpec(memory_space=pltpu.HBM)
    shape = jax.ShapeDtypeStruct(positions.shape, F32)
    links = len(OFFSETS)
    return pl.pallas_call(
        kernel,
        out_shape=(shape, shape),
        in_specs=[hbm, hbm, hbm],
        out_specs=(vmem, vmem),
        scratch_shapes=[
            pltpu.VMEM(positions.shape, F32),
            pltpu.VMEM(positions.shape, F32),
            pltpu.SMEM(counts.shape, jnp.int32),
            pltpu.VMEM(EXT + (4, 128), F32),
            pltpu.VMEM(EXT + (1, 128), F32),
            pltpu.VMEM((4, 6, 128, 32), BF16),
            pltpu.VMEM((COLUMNS, 6, 16, 256), BF16),
            pltpu.VMEM((CELLS, 32, 256), BF16),
            pltpu.VMEM((CELLS, 32, 512), BF16),
            pltpu.VMEM((4, 128, 768), F32),
            pltpu.VMEM((CELLS, 1, 128), F32),
            pltpu.VMEM((GRAD_ROWS, 768), BF16),
            pltpu.VMEM((80, 128, 256), F32),
            pltpu.VMEM((80, 128, 256), F32),
            pltpu.VMEM((112, 128, 256), F32),
            pltpu.VMEM((112, 128, 256), F32),
            pltpu.VMEM((48, 128, 128), F32),
            pltpu.VMEM((48, 128, 128), F32),
            pltpu.VMEM((CELLS, 8, 128), F32),
            pltpu.VMEM((CELLS, 16, 128), F32),
            pltpu.SemaphoreType.DMA((3,)),
            pltpu.SemaphoreType.DMA((links,)),
            pltpu.SemaphoreType.DMA((links,)),
            pltpu.SemaphoreType.DMA((links,)),
            pltpu.SemaphoreType.DMA((links,)),
        ],
        compiler_params=pltpu.CompilerParams(
            collective_id=0, has_side_effects=True, vmem_limit_bytes=62 * 1024 * 1024
        ),
    )(positions, velocities, counts)


def solution(mesh):
    spec = P(None, "gx", "gy", "gz", None)
    return jax.shard_map(
        body,
        mesh=mesh,
        in_specs=(spec, spec, P("gx", "gy", "gz")),
        out_specs=(spec, spec),
        check_vma=False,
    )
```

```python
import functools
import math

import jax
import jax.numpy as jnp
from jax import lax
from jax.experimental import pallas as pl
from jax.experimental.pallas import tpu as pltpu
from jax.sharding import PartitionSpec as P

MESH = pl.DeviceIdType.MESH
EDGE = 11.0
LOG2E = math.log2(math.e)
PEAK = 25.0 / 4.0
DEAD = -30000.0
RHO_SCALE = 0.4 * math.exp(-PEAK) / PEAK**2
FORCE_SCALE = 2.0 * -0.15 * math.exp(-2.0 * PEAK) / PEAK**2
GRAD_SCALE = 2.0 / 3.0 * math.exp(PEAK)
TIME_STEP = 0.5
OFFSETS = [
    (dx, dy, dz)
    for dx in (-1, 0, 1)
    for dy in (-1, 0, 1)
    for dz in (-1, 0, 1)
    if (dx, dy, dz) != (0, 0, 0)
]
OWN = (2, 2, 4)
EXT = (4, 4, 6)
CELLS = OWN[0] * OWN[1] * OWN[2]
COLUMNS = EXT[0] * EXT[1]
GRAD_ROWS = 8 * EXT[2]
F32, BF16 = jnp.float32, jnp.bfloat16


def source_slice(step, size):
    if step == 0:
        return pl.ds(1, size)
    return pl.ds(size if step > 0 else 1, 1)


def target_slice(step, size):
    if step == 0:
        return pl.ds(1, size)
    return pl.ds(0 if step > 0 else size + 1, 1)


def round16(value):
    return value.astype(BF16).astype(F32)


def split3(value):
    high = round16(value)
    rest = value - high
    low = round16(rest)
    return high, low, rest - low


def kernel(
    pos_hbm, vel_hbm, cnt_hbm, vout_ref, mout_ref,
    pos_ref, vel_ref, cnt_ref, ext, gext, lhs, mom, wts, pwts, gwide, grow, spread, own_p, own_r, wide_p, wide_r, single_p, single_r, dens, push,
    load_sem, send_sem, recv_sem, gsend_sem, grecv_sem,
):
    loads = [
        pltpu.make_async_copy(source, target, load_sem.at[k])
        for k, (source, target) in enumerate(
            ((pos_hbm, pos_ref), (cnt_hbm, cnt_ref), (vel_hbm, vel_ref))
        )
    ]
    for load in loads:
        load.start()

    sizes = [lax.axis_size(name) for name in ("gx", "gy", "gz")]
    me = [lax.axis_index(name) for name in ("gx", "gy", "gz")]

    def neighbour(offset):
        return tuple(lax.rem(m + d + n, n) for m, d, n in zip(me, offset, sizes))

    barrier = pltpu.get_barrier_semaphore()
    for offset in OFFSETS:
        pl.semaphore_signal(barrier, inc=1, device_id=neighbour(offset), device_id_type=MESH)

    for load in loads:
        load.wait()
    lane = lax.broadcasted_iota(jnp.int32, (1, 128), 1)
    for x in range(OWN[0]):
        for y in range(OWN[1]):
            for z in range(OWN[2]):
                for c in range(3):
                    ext[1 + x, 1 + y, 1 + z, c : c + 1, :] = (
                        pos_ref[c, x, y, z : z + 1, :] - 0.5 * EDGE
                    )
                live = jnp.where(lane < cnt_ref[x, y, z], 1.0, 0.0)
                ext[1 + x, 1 + y, 1 + z, 3:4, :] = live

    pl.semaphore_wait(barrier, len(OFFSETS))

    def exchange(buffer, sends, recvs):
        copies = []
        for k, offset in enumerate(OFFSETS):
            src = tuple(source_slice(d, n) for d, n in zip(offset, OWN))
            dst = tuple(target_slice(d, n) for d, n in zip(offset, OWN))
            copy = pltpu.make_async_remote_copy(
                src_ref=buffer.at[src],
                dst_ref=buffer.at[dst],
                send_sem=sends.at[k],
                recv_sem=recvs.at[k],
                device_id=neighbour(offset),
                device_id_type=MESH,
            )
            copy.start()
            copies.append(copy)
        return copies

    copies = exchange(ext, send_sem, recv_sem)
    row4 = lax.broadcasted_iota(jnp.int32, (4, 128), 0)

    def by_row(values):
        result = jnp.zeros((4, 128), F32)
        for k, value in enumerate(values):
            result = jnp.where(row4 == k, value, result)
        return result

    def shifted(x, y, z):
        cx = (x - 1.5) * EDGE
        cy = (y - 1.5) * EDGE
        cz = (z - 2.5) * EDGE
        return ext[x, y, z] + by_row((cx, cy, cz))

    def norm_of(point):
        square = point * point
        total = square[0:1] + square[1:2] + square[2:3]
        return jnp.where(point[3:4] > 0.5, -0.25 * total, DEAD)

    def expand(x, y, z):
        point = shifted(x, y, z)
        norm = norm_of(point)
        high, low, rest = split3(jnp.where(row4 == 3, norm, point))
        ones = jnp.ones_like(high)
        stack = jnp.concatenate([high, high, high, low, low, rest, ones, jnp.zeros_like(ones)], axis=0)
        moments = jnp.concatenate([high, low, rest, ones], axis=0).astype(BF16)
        mom[x * 4 + y, z] = jnp.concatenate([moments, moments], axis=1)
        return point, norm, stack.T.astype(BF16)

    def pair_columns(k):
        side = lax.rem(k, 2)
        return jnp.where(k < 2, 2 * side, side), jnp.where(k < 2, 2 * side + 1, side + 2)

    def own_column(q):
        return 1 + q // 2, 1 + lax.rem(q, 2)

    def own_step(q, carry):
        x, y = own_column(q)
        for z in range(4):
            point, norm, left = expand(x, y, z + 1)
            lhs[q, z + 1] = left
            blocks = []
            for unit in (LOG2E, 1.0):
                high, low, rest = split3(jnp.where(row4 == 3, unit, (0.5 * unit) * point))
                pieces = by_row(split3(unit * (norm + PEAK)))
                blocks.append(
                    jnp.concatenate(
                        [high, low, rest, high, low, high, pieces, jnp.zeros_like(pieces)], axis=0
                    )
                )
            wts[q * 4 + z] = jnp.concatenate(blocks, axis=1).astype(BF16)
        return carry

    lax.fori_loop(0, 4, own_step, 0)

    def pair_step(k, carry):
        first, second = pair_columns(k)
        for z in range(4):
            one, two = wts[first * 4 + z], wts[second * 4 + z]
            pwts[k * 4 + z] = jnp.concatenate(
                [one[:, 0:128], two[:, 0:128], one[:, 128:256], two[:, 128:256]], axis=1
            )
        return carry

    lax.fori_loop(0, 4, pair_step, 0)

    eye = lax.broadcasted_iota(jnp.int32, (128, 128), 0) == lax.broadcasted_iota(jnp.int32, (128, 128), 1)
    own_pairs = [(iz, jz) for iz in range(4) for jz in range(1, 5) if abs(iz + 1 - jz) <= 1]
    edge_pairs = [(0, 0), (3, 5)]
    all_pairs = [(iz, iz + dz) for iz in range(4) for dz in range(3)]

    def density_tile(left, weight, masked, stores, slot):
        both = jnp.dot(left, weight, preferred_element_type=F32)
        width = both.shape[1] // 2
        fall = jnp.exp2(both[:, 0:width])
        remain = jnp.maximum(both[:, width:], 0.0)
        if masked is not None:
            halves = [remain[:, h * 128 : h * 128 + 128] for h in range(width // 128)]
            halves[masked] = jnp.where(eye, 0.0, halves[masked])
            remain = jnp.concatenate(halves, axis=1)
        part = remain * fall
        rho = part * remain
        mixed = rho + part
        stores[0][slot] = mixed * fall
        stores[1][slot] = mixed + part
        return jnp.sum(rho.reshape(16, 8, width), axis=0)

    def force_tile(j, other, grad, stores, slot):
        if grad.shape[1] == 256:
            other = jnp.concatenate([other, other], axis=1)
        factor = stores[0][slot] + stores[1][slot] * (other + grad)
        high = factor.astype(BF16)
        low = (factor - high.astype(F32)).astype(BF16)
        return jnp.dot(mom[j], jnp.concatenate([high, low], axis=0), preferred_element_type=F32)

    row8 = lax.broadcasted_iota(jnp.int32, (8, 128), 0)

    def grad_column(x, y, inside):
        rows = []
        for z in range(6):
            if z not in inside:
                rows.append(jnp.zeros((8, 128), F32))
                continue
            high, low, rest = split3(GRAD_SCALE * gext[x, y, z])
            rows.append(
                jnp.where(row8 == 0, high, jnp.where(row8 == 1, low, jnp.where(row8 == 2, rest, 0.0)))
            )
        turned = jnp.concatenate(rows, axis=0).T.astype(BF16)
        return jnp.dot(turned, spread[...], preferred_element_type=F32)

    def own_index(column):
        if isinstance(column, int):
            return (column // 4 - 1) * 2 + column % 4 - 1
        return (column // 4 - 1) * 2 + lax.rem(column, 4) - 1

    def own_cells(kind, column):
        if kind == "density":
            return lambda z: lhs[own_index(column), z]
        return lambda z: gwide[own_index(column), :, z * 128 : z * 128 + 128]

    def halo_cells(kind, column):
        x, y = column // 4, lax.rem(column, 4)
        if kind == "density":
            lefts = [expand(x, y, z)[2] for z in range(6)]
            return lambda z: lefts[z]
        wide_grad = grad_column(x, y, range(6))
        return lambda z: wide_grad[:, z * 128 : z * 128 + 128]

    def group(kind, bases, weights, cells, items, stores, slot, first=False):
        totals = {}
        for n, (column, iz, jz, masked, *place) in enumerate(items):
            if kind == "density":
                part = density_tile(cells(column)(jz), weights(iz), masked, stores, slot + n)
            else:
                grad = jnp.concatenate([grow[base + iz] for base in bases], axis=1)
                part = force_tile(((place or [column])[0], jz), cells(column)(jz), grad, stores, slot + n)
            totals[iz] = part if iz not in totals else totals[iz] + part
        target = dens if kind == "density" else push
        for iz, total in totals.items():
            for h, base in enumerate(bases):
                block = total[:, h * 128 : h * 128 + 128]
                target[base + iz] = block if first else target[base + iz] + block

    def pair_group(kind, k, cells, items, stores, slot, first=False):
        one, two = pair_columns(k)
        group(kind, [one * 4, two * 4], lambda iz: pwts[k * 4 + iz], cells, items, stores, slot, first)

    def own_part(kind):
        def same_step(k, carry):
            columns = [(1 + k) * 4 + y for y in (1, 2)]
            items = [
                (column, iz, jz, h if jz == iz + 1 else None)
                for h, column in enumerate(columns)
                for iz, jz in own_pairs
            ]
            pair_group(kind, k, lambda c: own_cells(kind, c), items, [own_p, own_r], k * 20, True)
            return carry

        def other_step(p, carry):
            k = p // 2
            column = (2 - k) * 4 + 1 + lax.rem(p, 2)
            items = [(column, iz, jz, None) for iz, jz in own_pairs]
            pair_group(kind, k, lambda c: own_cells(kind, c), items, [own_p, own_r], 40 + p * 10)
            return carry

        lax.fori_loop(0, 2, same_step, 0)
        lax.fori_loop(0, 4, other_step, 0)

    def halo_part(kind):
        def face_step(k, carry):
            side = 1 + lax.rem(k, 2)
            near = k < 2
            cells, items = {}, []
            for far in range(2):
                column = jnp.where(
                    near, 4 * (3 * (side - 1)) + 1 + far, 4 * (1 + far) + 3 * (side - 1)
                )
                cells[far] = halo_cells(kind, column)
                items += [(far, iz, jz, None, column) for iz, jz in all_pairs]
            edge, half = k // 2, lax.rem(k, 2)
            edges = [(4 * (1 + half) + c, iz, jz, None) for c in (1, 2) for iz, jz in edge_pairs]
            pair_group(
                kind, edge, lambda c: own_cells(kind, c), edges, [wide_p, wide_r], edge * 8 + half * 4
            )
            corner = 12 * (k // 2) + 3 * side - 3
            corner_cells = halo_cells(kind, corner)
            pair_group(kind, k, lambda c: cells[c], items, [wide_p, wide_r], 16 + k * 24)
            group(
                kind, [k * 4], lambda iz: wts[k * 4 + iz], lambda c: corner_cells,
                [(corner, iz, jz, None) for iz, jz in all_pairs], [single_p, single_r], k * 12,
            )
            return carry

        lax.fori_loop(0, 4, face_step, 0)

    own_part("density")

    for copy in copies:
        copy.wait()

    for q in range(4):
        for z in (0, 5):
            lhs[q, z] = expand(1 + q // 2, 1 + q % 2, z)[2]

    halo_part("density")

    for q in range(4):
        x, y = 1 + q // 2, 1 + q % 2
        for z in range(4):
            density = RHO_SCALE * jnp.sum(dens[q * 4 + z], axis=0, keepdims=True)
            gext[x, y, z + 1] = ext[x, y, z + 1, 3:4, :] * 2.0 * (density - 1.0)

    copies = exchange(gext, gsend_sem, grecv_sem)

    spread_row = lax.broadcasted_iota(jnp.int32, (GRAD_ROWS, 768), 0) // 8
    spread_lane = lax.broadcasted_iota(jnp.int32, (GRAD_ROWS, 768), 1) // 128
    spread[...] = jnp.where(spread_row == spread_lane, 1.0, 0.0).astype(BF16)

    for q in range(4):
        for z in range(4):
            grow[q * 4 + z] = GRAD_SCALE * gext[1 + q // 2, 1 + q % 2, z + 1]
        gwide[q] = grad_column(1 + q // 2, 1 + q % 2, range(1, 5))

    own_part("force")

    for copy in copies:
        copy.wait()

    for q in range(4):
        edges = grad_column(1 + q // 2, 1 + q % 2, (0, 5))
        gwide[q, :, 0:128] = edges[:, 0:128]
        gwide[q, :, 640:768] = edges[:, 640:768]

    halo_part("force")

    for q in range(4):
        x, y = 1 + q // 2, 1 + q % 2
        for z in range(4):
            total = push[q * 4 + z]
            point = shifted(x, y, z + 1)
            live = point[3:4]
            force = FORCE_SCALE * (total[0:4] + total[4:8] + total[8:12] - point * total[12:13])
            for c in range(3):
                place = pos_ref[c, x - 1, y - 1, z : z + 1, :]
                velocity = vel_ref[c, x - 1, y - 1, z : z + 1, :] + TIME_STEP * force[c : c + 1]
                vout_ref[c, x - 1, y - 1, z : z + 1, :] = velocity * live
                mout_ref[c, x - 1, y - 1, z : z + 1, :] = (
                    (place + TIME_STEP * velocity) - place
                ) * live


def body(positions, velocities, counts):
    vmem = pl.BlockSpec(memory_space=pltpu.VMEM)
    hbm = pl.BlockSpec(memory_space=pltpu.HBM)
    shape = jax.ShapeDtypeStruct(positions.shape, F32)
    links = len(OFFSETS)
    return pl.pallas_call(
        kernel,
        out_shape=(shape, shape),
        in_specs=[hbm, hbm, hbm],
        out_specs=(vmem, vmem),
        scratch_shapes=[
            pltpu.VMEM(positions.shape, F32),
            pltpu.VMEM(positions.shape, F32),
            pltpu.SMEM(counts.shape, jnp.int32),
            pltpu.VMEM(EXT + (4, 128), F32),
            pltpu.VMEM(EXT + (1, 128), F32),
            pltpu.VMEM((4, 6, 128, 32), BF16),
            pltpu.VMEM((COLUMNS, 6, 16, 256), BF16),
            pltpu.VMEM((CELLS, 32, 256), BF16),
            pltpu.VMEM((CELLS, 32, 512), BF16),
            pltpu.VMEM((4, 128, 768), F32),
            pltpu.VMEM((CELLS, 1, 128), F32),
            pltpu.VMEM((GRAD_ROWS, 768), BF16),
            pltpu.VMEM((80, 128, 256), F32),
            pltpu.VMEM((80, 128, 256), F32),
            pltpu.VMEM((112, 128, 256), F32),
            pltpu.VMEM((112, 128, 256), F32),
            pltpu.VMEM((48, 128, 128), F32),
            pltpu.VMEM((48, 128, 128), F32),
            pltpu.VMEM((CELLS, 8, 128), F32),
            pltpu.VMEM((CELLS, 16, 128), F32),
            pltpu.SemaphoreType.DMA((3,)),
            pltpu.SemaphoreType.DMA((links,)),
            pltpu.SemaphoreType.DMA((links,)),
            pltpu.SemaphoreType.DMA((links,)),
            pltpu.SemaphoreType.DMA((links,)),
        ],
        compiler_params=pltpu.CompilerParams(
            collective_id=0, has_side_effects=True, vmem_limit_bytes=62 * 1024 * 1024
        ),
    )(positions, velocities, counts)


def solution(mesh):
    spec = P(None, "gx", "gy", "gz", None)
    return jax.shard_map(
        body,
        mesh=mesh,
        in_specs=(spec, spec, P("gx", "gy", "gz")),
        out_specs=(spec, spec),
        check_vma=False,
    )
```

```python
import functools
import math

import jax
import jax.numpy as jnp
from jax import lax
from jax.experimental import pallas as pl
from jax.experimental.pallas import tpu as pltpu
from jax.sharding import PartitionSpec as P

MESH = pl.DeviceIdType.MESH
EDGE = 11.0
LOG2E = math.log2(math.e)
PEAK = 25.0 / 4.0
DEAD = -30000.0
RHO_SCALE = 0.4 * math.exp(-PEAK) / PEAK**2
FORCE_SCALE = 2.0 * -0.15 * math.exp(-2.0 * PEAK) / PEAK**2
GRAD_SCALE = 2.0 / 3.0 * math.exp(PEAK)
TIME_STEP = 0.5
OFFSETS = [
    (dx, dy, dz)
    for dx in (-1, 0, 1)
    for dy in (-1, 0, 1)
    for dz in (-1, 0, 1)
    if (dx, dy, dz) != (0, 0, 0)
]
OWN = (2, 2, 4)
EXT = (4, 4, 6)
CELLS = OWN[0] * OWN[1] * OWN[2]
COLUMNS = EXT[0] * EXT[1]
GRAD_ROWS = 8 * EXT[2]
F32, BF16 = jnp.float32, jnp.bfloat16


def source_slice(step, size):
    if step == 0:
        return pl.ds(1, size)
    return pl.ds(size if step > 0 else 1, 1)


def target_slice(step, size):
    if step == 0:
        return pl.ds(1, size)
    return pl.ds(0 if step > 0 else size + 1, 1)


def round16(value):
    return value.astype(BF16).astype(F32)


def split3(value):
    high = round16(value)
    rest = value - high
    low = round16(rest)
    return high, low, rest - low


def kernel(
    pos_hbm, vel_hbm, cnt_hbm, vout_ref, mout_ref,
    pos_ref, vel_ref, cnt_ref, ext, gext, lhs, mom, wts, pwts, gwide, grow, spread, own_p, own_r, wide_p, wide_r, single_p, single_r, dens, push,
    load_sem, send_sem, recv_sem, gsend_sem, grecv_sem,
):
    loads = [
        pltpu.make_async_copy(source, target, load_sem.at[k])
        for k, (source, target) in enumerate(
            ((pos_hbm, pos_ref), (cnt_hbm, cnt_ref), (vel_hbm, vel_ref))
        )
    ]
    for load in loads:
        load.start()

    sizes = [lax.axis_size(name) for name in ("gx", "gy", "gz")]
    me = [lax.axis_index(name) for name in ("gx", "gy", "gz")]

    def neighbour(offset):
        return tuple(lax.rem(m + d + n, n) for m, d, n in zip(me, offset, sizes))

    barrier = pltpu.get_barrier_semaphore()
    for offset in OFFSETS:
        pl.semaphore_signal(barrier, inc=1, device_id=neighbour(offset), device_id_type=MESH)

    for load in loads:
        load.wait()
    lane = lax.broadcasted_iota(jnp.int32, (1, 128), 1)
    for x in range(OWN[0]):
        for y in range(OWN[1]):
            for z in range(OWN[2]):
                for c in range(3):
                    ext[1 + x, 1 + y, 1 + z, c : c + 1, :] = (
                        pos_ref[c, x, y, z : z + 1, :] - 0.5 * EDGE
                    )
                live = jnp.where(lane < cnt_ref[x, y, z], 1.0, 0.0)
                ext[1 + x, 1 + y, 1 + z, 3:4, :] = live

    pl.semaphore_wait(barrier, len(OFFSETS))

    def exchange(buffer, sends, recvs):
        copies = []
        for k, offset in enumerate(OFFSETS):
            src = tuple(source_slice(d, n) for d, n in zip(offset, OWN))
            dst = tuple(target_slice(d, n) for d, n in zip(offset, OWN))
            copy = pltpu.make_async_remote_copy(
                src_ref=buffer.at[src],
                dst_ref=buffer.at[dst],
                send_sem=sends.at[k],
                recv_sem=recvs.at[k],
                device_id=neighbour(offset),
                device_id_type=MESH,
            )
            copy.start()
            copies.append(copy)
        return copies

    copies = exchange(ext, send_sem, recv_sem)
    row4 = lax.broadcasted_iota(jnp.int32, (4, 128), 0)

    def by_row(values):
        result = jnp.zeros((4, 128), F32)
        for k, value in enumerate(values):
            result = jnp.where(row4 == k, value, result)
        return result

    def shifted(x, y, z):
        cx = (x - 1.5) * EDGE
        cy = (y - 1.5) * EDGE
        cz = (z - 2.5) * EDGE
        return ext[x, y, z] + by_row((cx, cy, cz))

    def norm_of(point):
        square = point * point
        total = square[0:1] + square[1:2] + square[2:3]
        return jnp.where(point[3:4] > 0.5, -0.25 * total, DEAD)

    def expand(x, y, z):
        point = shifted(x, y, z)
        norm = norm_of(point)
        high, low, rest = split3(jnp.where(row4 == 3, norm, point))
        ones = jnp.ones_like(high)
        stack = jnp.concatenate([high, high, high, low, low, rest, ones, jnp.zeros_like(ones)], axis=0)
        moments = jnp.concatenate([high, low, rest, ones], axis=0).astype(BF16)
        mom[x * 4 + y, z] = jnp.concatenate([moments, moments], axis=1)
        return point, norm, stack.T.astype(BF16)

    def pair_columns(k):
        side = lax.rem(k, 2)
        return jnp.where(k < 2, 2 * side, side), jnp.where(k < 2, 2 * side + 1, side + 2)

    def own_column(q):
        return 1 + q // 2, 1 + lax.rem(q, 2)

    def own_step(q, carry):
        x, y = own_column(q)
        for z in range(4):
            point, norm, left = expand(x, y, z + 1)
            lhs[q, z + 1] = left
            blocks = []
            for unit in (LOG2E, 1.0):
                high, low, rest = split3(jnp.where(row4 == 3, unit, (0.5 * unit) * point))
                pieces = by_row(split3(unit * (norm + PEAK)))
                blocks.append(
                    jnp.concatenate(
                        [high, low, rest, high, low, high, pieces, jnp.zeros_like(pieces)], axis=0
                    )
                )
            wts[q * 4 + z] = jnp.concatenate(blocks, axis=1).astype(BF16)
        return carry

    lax.fori_loop(0, 4, own_step, 0)

    def pair_step(k, carry):
        first, second = pair_columns(k)
        for z in range(4):
            one, two = wts[first * 4 + z], wts[second * 4 + z]
            pwts[k * 4 + z] = jnp.concatenate(
                [one[:, 0:128], two[:, 0:128], one[:, 128:256], two[:, 128:256]], axis=1
            )
        return carry

    lax.fori_loop(0, 4, pair_step, 0)

    eye = lax.broadcasted_iota(jnp.int32, (128, 128), 0) == lax.broadcasted_iota(jnp.int32, (128, 128), 1)
    own_pairs = [(iz, jz) for iz in range(4) for jz in range(1, 5) if abs(iz + 1 - jz) <= 1]
    edge_pairs = [(0, 0), (3, 5)]
    all_pairs = [(iz, iz + dz) for iz in range(4) for dz in range(3)]

    def density_tile(left, weight, masked, stores, slot):
        both = jnp.dot(left, weight, preferred_element_type=F32)
        width = both.shape[1] // 2
        fall = jnp.exp2(both[:, 0:width])
        remain = jnp.maximum(both[:, width:], 0.0)
        if masked is not None:
            halves = [remain[:, h * 128 : h * 128 + 128] for h in range(width // 128)]
            halves[masked] = jnp.where(eye, 0.0, halves[masked])
            remain = jnp.concatenate(halves, axis=1)
        part = remain * fall
        rho = part * remain
        mixed = rho + part
        stores[0][slot] = mixed * fall
        stores[1][slot] = mixed + part
        return jnp.sum(rho.reshape(16, 8, width), axis=0)

    def force_tile(j, other, grad, stores, slot):
        if grad.shape[1] == 256:
            other = jnp.concatenate([other, other], axis=1)
        factor = stores[0][slot] + stores[1][slot] * (other + grad)
        high = factor.astype(BF16)
        low = (factor - high.astype(F32)).astype(BF16)
        return jnp.dot(mom[j], jnp.concatenate([high, low], axis=0), preferred_element_type=F32)

    row8 = lax.broadcasted_iota(jnp.int32, (8, 128), 0)

    def grad_turned(x, y, inside):
        rows = []
        for z in range(6):
            if z not in inside:
                rows.append(jnp.zeros((8, 128), F32))
                continue
            high, low, rest = split3(GRAD_SCALE * gext[x, y, z])
            rows.append(
                jnp.where(row8 == 0, high, jnp.where(row8 == 1, low, jnp.where(row8 == 2, rest, 0.0)))
            )
        return jnp.concatenate(rows, axis=0).T.astype(BF16)

    def grad_column(x, y, inside):
        return jnp.dot(grad_turned(x, y, inside), spread[...], preferred_element_type=F32)

    def own_index(column):
        if isinstance(column, int):
            return (column // 4 - 1) * 2 + column % 4 - 1
        return (column // 4 - 1) * 2 + lax.rem(column, 4) - 1

    def own_cells(kind, column):
        if kind == "density":
            return lambda z: lhs[own_index(column), z]
        return lambda z: gwide[own_index(column), :, z * 128 : z * 128 + 128]

    def halo_cells(kind, column):
        x, y = column // 4, lax.rem(column, 4)
        if kind == "density":
            lefts = [expand(x, y, z)[2] for z in range(6)]
            return lambda z: lefts[z]
        wide_grad = grad_column(x, y, range(6))
        return lambda z: wide_grad[:, z * 128 : z * 128 + 128]

    def group(kind, bases, weights, cells, items, stores, slot, first=False):
        totals = {}
        for n, (column, iz, jz, masked, *place) in enumerate(items):
            if kind == "density":
                part = density_tile(cells(column)(jz), weights(iz), masked, stores, slot + n)
            else:
                grad = jnp.concatenate([grow[base + iz] for base in bases], axis=1)
                part = force_tile(((place or [column])[0], jz), cells(column)(jz), grad, stores, slot + n)
            totals[iz] = part if iz not in totals else totals[iz] + part
        target = dens if kind == "density" else push
        for iz, total in totals.items():
            for h, base in enumerate(bases):
                block = total[:, h * 128 : h * 128 + 128]
                target[base + iz] = block if first else target[base + iz] + block

    def pair_group(kind, k, cells, items, stores, slot, first=False):
        one, two = pair_columns(k)
        group(kind, [one * 4, two * 4], lambda iz: pwts[k * 4 + iz], cells, items, stores, slot, first)

    def own_part(kind):
        def same_step(k, carry):
            columns = [(1 + k) * 4 + y for y in (1, 2)]
            items = [
                (column, iz, jz, h if jz == iz + 1 else None)
                for h, column in enumerate(columns)
                for iz, jz in own_pairs
            ]
            pair_group(kind, k, lambda c: own_cells(kind, c), items, [own_p, own_r], k * 20, True)
            return carry

        def other_step(p, carry):
            k = p // 2
            column = (2 - k) * 4 + 1 + lax.rem(p, 2)
            items = [(column, iz, jz, None) for iz, jz in own_pairs]
            pair_group(kind, k, lambda c: own_cells(kind, c), items, [own_p, own_r], 40 + p * 10)
            return carry

        lax.fori_loop(0, 2, same_step, 0)
        lax.fori_loop(0, 4, other_step, 0)

    def halo_part(kind):
        def face_step(k, carry):
            side = 1 + lax.rem(k, 2)
            near = k < 2
            cells, items = {}, []
            for far in range(2):
                column = jnp.where(
                    near, 4 * (3 * (side - 1)) + 1 + far, 4 * (1 + far) + 3 * (side - 1)
                )
                cells[far] = halo_cells(kind, column)
                items += [(far, iz, jz, None, column) for iz, jz in all_pairs]
            edge, half = k // 2, lax.rem(k, 2)
            edges = [(4 * (1 + half) + c, iz, jz, None) for c in (1, 2) for iz, jz in edge_pairs]
            pair_group(
                kind, edge, lambda c: own_cells(kind, c), edges, [wide_p, wide_r], edge * 8 + half * 4
            )
            corner = 12 * (k // 2) + 3 * side - 3
            corner_cells = halo_cells(kind, corner)
            pair_group(kind, k, lambda c: cells[c], items, [wide_p, wide_r], 16 + k * 24)
            group(
                kind, [k * 4], lambda iz: wts[k * 4 + iz], lambda c: corner_cells,
                [(corner, iz, jz, None) for iz, jz in all_pairs], [single_p, single_r], k * 12,
            )
            return carry

        lax.fori_loop(0, 4, face_step, 0)

    own_part("density")

    for copy in copies:
        copy.wait()

    for q in range(4):
        for z in (0, 5):
            lhs[q, z] = expand(1 + q // 2, 1 + q % 2, z)[2]

    halo_part("density")

    for q in range(4):
        x, y = 1 + q // 2, 1 + q % 2
        for z in range(4):
            density = RHO_SCALE * jnp.sum(dens[q * 4 + z], axis=0, keepdims=True)
            gext[x, y, z + 1] = ext[x, y, z + 1, 3:4, :] * 2.0 * (density - 1.0)

    copies = exchange(gext, gsend_sem, grecv_sem)

    spread_row = lax.broadcasted_iota(jnp.int32, (GRAD_ROWS, 768), 0) // 8
    spread_lane = lax.broadcasted_iota(jnp.int32, (GRAD_ROWS, 768), 1) // 128
    spread[...] = jnp.where(spread_row == spread_lane, 1.0, 0.0).astype(BF16)

    for q in range(4):
        for z in range(4):
            grow[q * 4 + z] = GRAD_SCALE * gext[1 + q // 2, 1 + q % 2, z + 1]
        gwide[q] = grad_column(1 + q // 2, 1 + q % 2, range(1, 5))

    own_part("force")

    for copy in copies:
        copy.wait()

    for q in range(4):
        turned = grad_turned(1 + q // 2, 1 + q % 2, (0, 5))
        for lanes in (slice(0, 128), slice(640, 768)):
            gwide[q, :, lanes] = jnp.dot(turned, spread[:, lanes], preferred_element_type=F32)

    halo_part("force")

    for q in range(4):
        x, y = 1 + q // 2, 1 + q % 2
        for z in range(4):
            total = push[q * 4 + z]
            point = shifted(x, y, z + 1)
            live = point[3:4]
            force = FORCE_SCALE * (total[0:4] + total[4:8] + total[8:12] - point * total[12:13])
            for c in range(3):
                place = pos_ref[c, x - 1, y - 1, z : z + 1, :]
                velocity = vel_ref[c, x - 1, y - 1, z : z + 1, :] + TIME_STEP * force[c : c + 1]
                vout_ref[c, x - 1, y - 1, z : z + 1, :] = velocity * live
                mout_ref[c, x - 1, y - 1, z : z + 1, :] = (
                    (place + TIME_STEP * velocity) - place
                ) * live


def body(positions, velocities, counts):
    vmem = pl.BlockSpec(memory_space=pltpu.VMEM)
    hbm = pl.BlockSpec(memory_space=pltpu.HBM)
    shape = jax.ShapeDtypeStruct(positions.shape, F32)
    links = len(OFFSETS)
    return pl.pallas_call(
        kernel,
        out_shape=(shape, shape),
        in_specs=[hbm, hbm, hbm],
        out_specs=(vmem, vmem),
        scratch_shapes=[
            pltpu.VMEM(positions.shape, F32),
            pltpu.VMEM(positions.shape, F32),
            pltpu.SMEM(counts.shape, jnp.int32),
            pltpu.VMEM(EXT + (4, 128), F32),
            pltpu.VMEM(EXT + (1, 128), F32),
            pltpu.VMEM((4, 6, 128, 32), BF16),
            pltpu.VMEM((COLUMNS, 6, 16, 256), BF16),
            pltpu.VMEM((CELLS, 32, 256), BF16),
            pltpu.VMEM((CELLS, 32, 512), BF16),
            pltpu.VMEM((4, 128, 768), F32),
            pltpu.VMEM((CELLS, 1, 128), F32),
            pltpu.VMEM((GRAD_ROWS, 768), BF16),
            pltpu.VMEM((80, 128, 256), F32),
            pltpu.VMEM((80, 128, 256), F32),
            pltpu.VMEM((112, 128, 256), F32),
            pltpu.VMEM((112, 128, 256), F32),
            pltpu.VMEM((48, 128, 128), F32),
            pltpu.VMEM((48, 128, 128), F32),
            pltpu.VMEM((CELLS, 8, 128), F32),
            pltpu.VMEM((CELLS, 16, 128), F32),
            pltpu.SemaphoreType.DMA((3,)),
            pltpu.SemaphoreType.DMA((links,)),
            pltpu.SemaphoreType.DMA((links,)),
            pltpu.SemaphoreType.DMA((links,)),
            pltpu.SemaphoreType.DMA((links,)),
        ],
        compiler_params=pltpu.CompilerParams(
            collective_id=0, has_side_effects=True, vmem_limit_bytes=62 * 1024 * 1024
        ),
    )(positions, velocities, counts)


def solution(mesh):
    spec = P(None, "gx", "gy", "gz", None)
    return jax.shard_map(
        body,
        mesh=mesh,
        in_specs=(spec, spec, P("gx", "gy", "gz")),
        out_specs=(spec, spec),
        check_vma=False,
    )
```
